256 devices in a mesh: section: 16 (over y_hi, x, core), expert: 8 (over z), dp: 2 (over y_lo).
Axes of the slice: x: 4, y: 4 (y_hi: 2, y_lo: 2; y = y_hi * 2 + y_lo), z: 8, core: 2. Of those that a mesh axis runs over, the one named last changes fastest.
Arguments:
- held_states: bfloat16 [16, 2, 512, 3584], P('section', None, ('expert', 'dp')), may hold values from -6 to 6
- entering_rows: bfloat16 [1, 2, 512, 3584], P(None, None, ('expert', 'dp')), may hold values from -6 to 6
- norm_gain: bfloat16 [16, 3584], P('section'), may hold values from 0.5 to 1.5
- router_weight: bfloat16 [16, 8, 3584], P('section'), may hold values from -0.1875 to 0.1875
- up_weight: bfloat16 [16, 8, 3584, 1024], P('section', 'expert', None, 'dp'), may hold values from -0.09375 to 0.09375
- down_weight: bfloat16 [16, 8, 1024, 3584], P('section', 'expert', 'dp'), may hold values from -0.1875 to 0.1875
- expert_routes: int32 [16, 2, 2, 512, 2], P('section', None, None, 'expert'), may hold values from 0 to 7, all different within a row; in each aligned block of 32 rows (0 to 31, 32 to 63, ..., all dimensions but the last counted through in order) at most 12 rows name the same one
- weight_cotangent: float32 [16, 2, 2, 512, 2], P('section', None, None, ('expert', 'dp')), may hold values from -6 to 6
Outputs:
- layer_out: bfloat16 [16, 2, 2, 512, 3584], P('section', None, None, ('expert', 'dp'))
- router_grads: float32 [16, 8, 3584], P('section', None, ('expert', 'dp'))
The draws below stay inside these ranges and needn't reach their ends.
Inputs may be any that keep to these rules, and one draw needn't show every extreme that they name: `expert_routes`: each token names 2 different experts. In each aligned block of 32 tokens (the tokens of one device) no expert is named by more than 12 routes, a bound that some block reaches.
All inputs are finite; a program needn't handle non-finite values.
Results may differ from the reference program's by a relative error of at most 0.022.
Values may be sent and summed in bfloat16 or wider, within the bound.
A program may use at most 64 MiB of HBM per device.

```python
import math
import jax
import jax.numpy as jnp
import numpy as np
from jax import lax

D = 3584
FF = 1024
K = 2
TICKS = 2
TOK_DEV = 32
LAYERS = 16
EXPERTS = 8
TOKENS = 512
CAP = 12
N_DP = 2


def block_scale(rng, dims, shards, low, high):
    level = 1.0
    for axis_at, blocks in shards:
        heights = jax.random.uniform(jax.random.fold_in(jax.random.fold_in(rng, 6), axis_at), (blocks,), jnp.float32, low / len(shards), high / len(shards))
        level = level * jnp.repeat(jnp.exp(heights), dims[axis_at] // blocks).reshape((-1,) + (1,) * (len(dims) - 1 - axis_at))
    return level


def shared_out(key, own, number, rows, count, top, most, skew):
    ranking = jax.random.permutation(key, count)
    crowded, common = shares(count, rows * top, most, skew, True), shares(count, rows * top, most, skew, False)
    places = jnp.arange(count)

    def named(sizes, turn):
        used = int((sizes > 0).sum())
        fixed = max(1, used // 4)
        passed = fixed + (places - fixed + turn * (used - fixed)) % max(1, count - fixed)
        return jnp.zeros((count,), jnp.int32).at[ranking[jnp.where(places < fixed, places, passed)]].set(jnp.asarray(sizes, jnp.int32))

    sizes = jnp.where(number % 4 == 0, named(crowded, number // 4), named(common, number - number // 4 - 1))
    mixed = jax.random.permutation(jax.random.fold_in(own, 3), count)
    donor, receiver = mixed[0:count // 2 * 2:2], mixed[1:count // 2 * 2:2]
    margin = jnp.minimum(sizes[donor] - 1, most - sizes[receiver]) // 2
    margin = jnp.where((donor == ranking[0]) | (receiver == ranking[0]) | (sizes[receiver] == 0), 0, jnp.maximum(margin, 0))
    passed = jax.random.randint(jax.random.fold_in(own, 4), (count // 2,), 0, 1 << 20) % (margin + 1)
    sizes = sizes.at[donor].add(-passed).at[receiver].add(passed)
    items = jnp.searchsorted(jnp.cumsum(sizes), jnp.arange(rows * top), side="right").astype(jnp.int32)
    table = items.reshape(top, rows).T
    table = table[jax.random.permutation(jax.random.fold_in(own, 1), rows)]
    turn = jax.random.randint(jax.random.fold_in(own, 2), (rows, 1), 0, top)
    return jnp.take_along_axis(table, (jnp.arange(top)[None, :] + turn) % top, axis=1)


def shares(count, total, most, skew, full):
    loads = [(1 << 20) // math.isqrt(grade ** skew) + 1 for grade in range(1, count + 1)]
    largest = most if full else min(most, max(-(-total // count), total * loads[0] // sum(loads)))
    least = 1 if total - largest >= count - 1 else 0
    counts, surplus = [largest] + [least] * (count - 1), total - largest - least * (count - 1)
    while surplus > 0:
        candidates = [i for i in range(1, count) if counts[i] < largest] or [i for i in range(1, count) if counts[i] < most]
        whole, budget = sum([loads[i] for i in candidates]), surplus
        for i in candidates:
            addition = min(most - counts[i], max(1, budget * loads[i] // whole), surplus)
            counts[i] = counts[i] + addition
            surplus = surplus - addition
    return np.array(counts)


def bell_draw(key, shape, spread, limit, shards=(), kind=jnp.bfloat16):
    array = jax.random.normal(key, shape, jnp.float32) * spread
    if len(shards) > 0:
        array = block_scale(key, shape, shards, -0.22, 0.18) * array
    return jnp.clip(array, min=-limit, max=limit).astype(kind)


def setup_inputs(seed: int = 0) -> dict:
    seeds = jax.random.split(jax.random.key(seed), 9)
    held_states = bell_draw(seeds[0], (LAYERS, 2, TOKENS, D), 1.0, 6.0, ((0, 16), (2, 16)))
    entering_rows = bell_draw(seeds[1], (TICKS - 1, 2, TOKENS, D), 1.0, 6.0, ((2, 16),))
    norm_gain = jnp.clip(1.0 + 0.1 * jax.random.normal(seeds[2], (LAYERS, D), jnp.float32), 0.5, 1.5).astype(jnp.bfloat16)
    router_weight = bell_draw(seeds[3], (LAYERS, EXPERTS, D), (D // 4) ** -0.5, 0.1875, ((0, 16),))
    up_weight = bell_draw(seeds[4], (LAYERS, EXPERTS, D, FF), D ** -0.5, 0.09375, ((0, 16), (1, 8), (3, 2)))
    down_weight = bell_draw(seeds[5], (LAYERS, EXPERTS, FF, D), FF ** -0.5, 0.1875, ((0, 16), (1, 8), (2, 2)))
    expert_routes_keys = jax.random.split(jax.random.fold_in(seeds[6], 1), LAYERS * TICKS * 2 * TOKENS // TOK_DEV)
    expert_routes_turns = jax.random.permutation(jax.random.fold_in(seeds[6], 3), LAYERS * TICKS * 2 * TOKENS // TOK_DEV)
    expert_routes = jax.vmap(lambda own, number: shared_out(jax.random.fold_in(seeds[6], 2), own, number, TOK_DEV, EXPERTS, K, CAP, 2))(expert_routes_keys, expert_routes_turns).reshape((LAYERS, TICKS, 2, TOKENS, K))
    weight_cotangent = bell_draw(seeds[7], (LAYERS, TICKS, 2, TOKENS, K), 1.0, 6.0, ((0, 16), (3, 16)), jnp.float32)
    return dict(held_states=held_states, entering_rows=entering_rows, norm_gain=norm_gain, router_weight=router_weight, up_weight=up_weight, down_weight=down_weight, expert_routes=expert_routes, weight_cotangent=weight_cotangent)


route_scale = 2.5

def normalize(tokens_in, gain_row):
    values = tokens_in.astype(jnp.float32)
    meansq = lax.optimization_barrier(jnp.mean(values * values, axis=-1, keepdims=True))
    return (values * lax.rsqrt(meansq + 1e-06) * gain_row.astype(jnp.float32)).astype(jnp.bfloat16)

def gating(normed, router_rows, own_routes, expert_count):
    logits = jnp.dot(normed, router_rows.T, preferred_element_type=jnp.float32)
    route_hot = (own_routes[:, :, None] == jnp.arange(expert_count, dtype=jnp.int32)).astype(jnp.float32)
    picked = lax.optimization_barrier(jnp.sum(logits[:, None, :] * route_hot, axis=2))
    affinity = jax.nn.sigmoid(picked)
    aff_total = lax.optimization_barrier(jnp.sum(affinity, axis=1, keepdims=True))
    weights = route_scale * affinity / aff_total
    return (weights, affinity, aff_total, route_hot)

def router_grad(normed, affinity, aff_total, route_hot, cotangent):
    inner_sum = lax.optimization_barrier(jnp.sum(cotangent * affinity, axis=1, keepdims=True))
    aff_grad = route_scale * (cotangent / aff_total - inner_sum / (aff_total * aff_total))
    logit_grad = aff_grad * affinity * (1.0 - affinity)
    dense_grad = lax.optimization_barrier(jnp.sum(logit_grad[:, :, None] * route_hot, axis=1))
    return jnp.dot(dense_grad.T, normed.astype(jnp.float32), precision=lax.Precision.HIGHEST, preferred_element_type=jnp.float32)

def slot_index(block_routes, expert_count):
    block_count = block_routes.shape[0]
    flat_rows = block_routes.reshape(block_count, -1)
    route_hot = (flat_rows[:, :, None] == jnp.arange(expert_count, dtype=jnp.int32)).astype(jnp.int32)
    earlier = jnp.cumsum(route_hot, axis=1) - route_hot
    return lax.optimization_barrier(jnp.sum(earlier * route_hot, axis=2)).astype(jnp.int32).reshape(block_routes.shape)

def expert_part(flat_rows, up_local, down_local):
    pre_act = jnp.dot(flat_rows, up_local, preferred_element_type=jnp.float32)
    hidden = jax.nn.silu(pre_act).astype(jnp.bfloat16)
    return jnp.dot(hidden, down_local, preferred_element_type=jnp.float32)

def section_layer(operands):
    tokens_in, gain_row, router_rows, up_all, down_all, routes_now, cotangent = operands
    normed = normalize(tokens_in, gain_row)
    weights, affinity, aff_total, route_hot = gating(normed, router_rows, routes_now, EXPERTS)
    grad_part = router_grad(normed, affinity, aff_total, route_hot, cotangent)
    block_count = TOKENS // TOK_DEV
    block_routes = routes_now.reshape(block_count, TOK_DEV, K)
    slot_rank = slot_index(block_routes, EXPERTS)
    block_ids = jnp.arange(block_count, dtype=jnp.int32)[:, None, None]
    slot_target = ((block_routes * block_count + block_ids) * CAP + slot_rank).reshape(-1).astype(jnp.int32)
    sources = jnp.repeat(normed, K, axis=0)
    buffer = jnp.zeros((EXPERTS * block_count * CAP, D), jnp.bfloat16).at[slot_target].set(sources)
    buffer = buffer.reshape(EXPERTS, block_count * CAP, D)
    half_width = FF // N_DP

    def one_expert(expert_ops):
        slot_rows, up_one, down_one = expert_ops
        summed = jnp.zeros((slot_rows.shape[0], D), jnp.float32)
        for half_index in range(N_DP):
            partial_value = expert_part(slot_rows, up_one[:, half_index * half_width:(half_index + 1) * half_width], down_one[half_index * half_width:(half_index + 1) * half_width, :])
            rounded = lax.optimization_barrier(partial_value.astype(jnp.bfloat16))
            summed = summed + rounded.astype(jnp.float32)
        return summed.astype(jnp.bfloat16)
    results = lax.map(one_expert, (buffer, up_all, down_all))
    gathered_back = results.reshape(-1, D)[slot_target].reshape(TOKENS, K, D)
    mixed = tokens_in.astype(jnp.float32) + lax.optimization_barrier(jnp.sum(weights[:, :, None] * gathered_back.astype(jnp.float32), axis=1))
    return (mixed.astype(jnp.bfloat16), grad_part)

def reference(held_states, entering_rows, norm_gain, router_weight, up_weight, down_weight, expert_routes, weight_cotangent):
    grads = jnp.zeros((LAYERS, EXPERTS, D), jnp.float32)
    state_a = held_states[:, 0]
    state_b = held_states[:, 1]
    per_tick = []
    for tick_step in range(TICKS):
        mixed_a, grad_a = lax.map(section_layer, (state_a, norm_gain, router_weight, up_weight, down_weight, expert_routes[:, tick_step, 0], weight_cotangent[:, tick_step, 0]))
        mixed_b, grad_b = lax.map(section_layer, (state_b, norm_gain, router_weight, up_weight, down_weight, expert_routes[:, tick_step, 1], weight_cotangent[:, tick_step, 1]))
        grads = grads + grad_a + grad_b
        per_tick.append(jnp.stack([mixed_a, mixed_b], axis=1))
        if tick_step + 1 < TICKS:
            state_a = jnp.concatenate([entering_rows[tick_step, 0][None], mixed_a[:-1]], axis=0)
            state_b = jnp.concatenate([mixed_b[1:], entering_rows[tick_step, 1][None]], axis=0)
    return (jnp.stack(per_tick, axis=1), grads)
```

```python
import functools

import jax
import jax.numpy as jnp
from jax import lax
from jax.experimental import pallas as pl
from jax.experimental.pallas import tpu as pltpu
from jax.sharding import PartitionSpec as P

TICKS = 2
UNITS = 4
D = 3584
TOK = 32
NE = 8
HALF = D // 2
QUART = D // 4
PACK = HALF + QUART
ROWS = NE * 16
PART = D // 16
SCALE = 2.5
MESH = pl.DeviceIdType.MESH
F32 = jnp.float32
BF16 = jnp.bfloat16
RING = (1, 7, 2, 6, 3, 5, 4)


def dot(a, b):
    return jnp.dot(a, b, preferred_element_type=F32)


def split_two(value):
    high = value.astype(BF16)
    return high, (value - high.astype(F32)).astype(BF16)


def kernel(
    held,
    entering,
    gain,
    router,
    up_hbm,
    down_hbm,
    routes,
    cot,
    out_hbm,
    grads,
    states,
    normed,
    up,
    down,
    packed,
    gath,
    part,
    yret,
    summed,
    back,
    outs,
    place,
    place_a,
    place_b,
    mix_a,
    mix_b,
    dense,
    gfull,
    gsend,
    grecv,
    gsum,
    gall,
    in_sem,
    out_sem,
    zs,
    zr,
    ys,
    yr,
    ss,
    sr,
    rs,
    rr,
    hs,
    hr,
    gs,
    gr,
):
    sec = lax.axis_index("section")
    me = lax.axis_index("expert")
    dp = lax.axis_index("dp")
    sections = lax.axis_size("section")

    def ring(offset):
        return lax.rem(me + offset + NE, NE)

    def block(index):
        return pl.ds(pl.multiple_of(index * 16, 16), 16)

    def other(index):
        return pl.ds(pl.multiple_of(index * 16 + ROWS, 16), 16)

    barrier = pltpu.get_barrier_semaphore()
    for offset in RING:
        pl.semaphore_signal(barrier, inc=1, device_id={"expert": ring(offset)}, device_id_type=MESH)
    pl.semaphore_signal(barrier, inc=1, device_id={"dp": 1 - dp}, device_id_type=MESH)

    @pl.when(sec > 0)
    def _():
        pl.semaphore_signal(barrier, inc=1, device_id={"section": sec - 1}, device_id_type=MESH)

    @pl.when(sec < sections - 1)
    def _():
        pl.semaphore_signal(barrier, inc=1, device_id={"section": sec + 1}, device_id_type=MESH)

    loads = [
        pltpu.make_async_copy(held.at[0, 0], states.at[0], in_sem.at[0]),
        pltpu.make_async_copy(held.at[0, 1], states.at[1], in_sem.at[1]),
        pltpu.make_async_copy(up_hbm.at[0, 0], up, in_sem.at[2]),
        pltpu.make_async_copy(down_hbm.at[0, 0], down, in_sem.at[3]),
    ]
    for load in loads:
        load.start()
    enter_up = pltpu.make_async_copy(entering.at[0, 0], states.at[2], in_sem.at[4])
    enter_down = pltpu.make_async_copy(entering.at[0, 1], states.at[3], in_sem.at[5])

    @pl.when(sec == 0)
    def _():
        enter_up.start()

    @pl.when(sec == sections - 1)
    def _():
        enter_down.start()

    def z_copy(u, i):
        to = ring(RING[i])
        return pltpu.make_async_remote_copy(
            src_ref=packed.at[u, block(to)],
            dst_ref=gath.at[u, block(me)],
            send_sem=zs.at[u, i],
            recv_sem=zr.at[u, i],
            device_id={"expert": to},
            device_id_type=MESH,
        )

    def origin(i):
        return me if i == 7 else ring(-RING[i])

    def y_copy(u, i):
        src = packed if i == 7 else gath
        return pltpu.make_async_remote_copy(
            src_ref=src.at[u, block(origin(i))],
            dst_ref=gath.at[u, other(origin(i))],
            send_sem=ys.at[u, i],
            recv_sem=yr.at[u, i],
            device_id={"dp": 1 - dp},
            device_id_type=MESH,
        )

    def target(i):
        return me if i == 7 else ring(RING[i])

    def s_copy(u, i):
        return pltpu.make_async_remote_copy(
            src_ref=part.at[u, other(target(i))],
            dst_ref=yret.at[u, block(target(i))],
            send_sem=ss.at[u, i],
            recv_sem=sr.at[u, i],
            device_id={"dp": 1 - dp},
            device_id_type=MESH,
        )

    def r_copy(u, i):
        to = ring(RING[i])
        return pltpu.make_async_remote_copy(
            src_ref=summed.at[u, block(to)],
            dst_ref=back.at[u, block(me)],
            send_sem=rs.at[u, i],
            recv_sem=rr.at[u, i],
            device_id={"expert": to},
            device_id_type=MESH,
        )

    def h_copy(d):
        return pltpu.make_async_remote_copy(
            src_ref=outs.at[d],
            dst_ref=states.at[2 + d],
            send_sem=hs.at[d],
            recv_sem=hr.at[d],
            device_id={"section": sec + 1 if d == 0 else sec - 1},
            device_id_type=MESH,
        )

    def g_copy(i):
        if i == 7:
            return pltpu.make_async_remote_copy(
                src_ref=gsend.at[1 - dp],
                dst_ref=grecv,
                send_sem=gs.at[7],
                recv_sem=gr.at[7],
                device_id={"dp": 1 - dp},
                device_id_type=MESH,
            )
        to = ring(RING[i])
        return pltpu.make_async_remote_copy(
            src_ref=gsum.at[to],
            dst_ref=gall.at[me],
            send_sem=gs.at[i],
            recv_sem=gr.at[i],
            device_id={"expert": to},
            device_id_type=MESH,
        )

    def rows_of(u):
        return slice(u * TOK, (u + 1) * TOK)

    def own_routes(u):
        return routes[0, u // 2, u % 2, pl.ds(pl.multiple_of(dp * TOK, TOK), TOK), :]

    def slots(u):
        chosen = own_routes(u)
        lane = lax.broadcasted_iota(jnp.int32, (TOK, ROWS), 1)
        expert, row = lane // 16, lane % 16
        hit = (chosen[:, 0:1] == expert) | (chosen[:, 1:2] == expert)
        earlier = lax.broadcasted_iota(jnp.int32, (TOK, TOK), 0) > lax.broadcasted_iota(
            jnp.int32, (TOK, TOK), 1
        )
        rank = dot(earlier.astype(F32).astype(BF16), hit.astype(F32).astype(BF16)).astype(jnp.int32)
        first = hit & (rank == row % 8)
        last = hit & (rank == 8 + row % 4)
        pa = jnp.concatenate([(first & (row // 8 == h)).astype(F32) for h in range(2)], axis=0)
        pb = jnp.concatenate([(last & (row // 4 == q)).astype(F32) for q in range(4)], axis=0)
        place[u, 0:64] = pa
        place[u, 64:192] = pb
        place_a[u] = pa.T.astype(BF16)
        place_b[u] = pb.T.astype(BF16)

    def norm(u):
        values = states[u].astype(F32)
        meansq = jnp.mean(values * values, axis=-1, keepdims=True)
        normed[rows_of(u)] = (
            values * lax.rsqrt(meansq + 1e-06) * gain[...].astype(F32)
        ).astype(BF16)

    def pack(u):
        own = normed[rows_of(u)]
        halves = jnp.concatenate([own[:, :HALF], own[:, HALF:]], axis=0)
        packed[u, :, 0:HALF] = dot(place_a[u], halves).astype(BF16)
        quarters = jnp.concatenate([own[:, q * QUART : (q + 1) * QUART] for q in range(4)], axis=0)
        packed[u, :, HALF:] = dot(place_b[u], quarters).astype(BF16)

    def dispatch(u):
        for i in range(7):
            z_copy(u, i).start()
        y_copy(u, 7).start()
        gath[u, block(me)] = packed[u, block(me)]

    def forward(u, i):
        z_copy(u, i).wait_recv()
        y_copy(u, i).start()

    def gate(u):
        chosen = own_routes(u)
        cotangent = cot[0, u // 2, u % 2]
        logits = lax.dot_general(
            normed[rows_of(u)], router[0], (((1,), (1,)), ((), ())), preferred_element_type=F32
        )
        lane = lax.broadcasted_iota(jnp.int32, (TOK, NE), 1)
        hit0, hit1 = chosen[:, 0:1] == lane, chosen[:, 1:2] == lane
        affinity = jnp.where(hit0 | hit1, jax.nn.sigmoid(logits), 0.0)
        total = jnp.sum(affinity, axis=1, keepdims=True)
        weights = SCALE * affinity / total
        cots = jnp.where(hit0, cotangent[:, 0:1], 0.0) + jnp.where(hit1, cotangent[:, 1:2], 0.0)
        inner = jnp.sum(cots * affinity, axis=1, keepdims=True)
        slope = SCALE * (cots / total - inner / (total * total))
        dense[rows_of(u)] = slope * affinity * (1.0 - affinity)
        expert = lax.broadcasted_iota(jnp.int32, (TOK, ROWS), 1) // 16
        spread = jnp.zeros((TOK, ROWS), F32)
        for e in range(NE):
            spread = jnp.where(expert == e, weights[:, e : e + 1], spread)
        high, low = split_two(spread)
        high, low = high.astype(F32), low.astype(F32)
        for h in range(6):
            hot = place[u, h * TOK : (h + 1) * TOK]
            both = jnp.concatenate([hot * high, hot * low], axis=0).astype(BF16)
            if h < 2:
                mix_a[u, h * 64 : (h + 1) * 64] = both
            else:
                mix_b[u, (h - 2) * 64 : (h - 1) * 64] = both

    def hidden(u):
        first = gath[u, :, 0:HALF]
        left = dot(first, up[0:HALF]).reshape(16, 2, 8, 512)
        right = dot(first, up[HALF:]).reshape(16, 2, 8, 512)
        pre_a = (left[:, 0] + right[:, 1]).reshape(128, 512)
        last = gath[u, :, HALF:]
        upper = lax.broadcasted_iota(jnp.int32, (16, 8, 512), 1) < 4
        quart = [
            dot(last, up[g * QUART : (g + 1) * QUART]).reshape(16, 2, 8, 512)[:, g // 2]
            for g in range(4)
        ]
        halves = jnp.where(upper, quart[0] + quart[2], quart[1] + quart[3])
        pre_b = (halves + pltpu.roll(halves, 4, 1)).reshape(128, 512)
        act_a = (pre_a * jax.nn.sigmoid(pre_a)).astype(BF16)
        act_b = (pre_b * jax.nn.sigmoid(pre_b)).astype(BF16)
        return act_a, act_b

    def project(u, act_a, act_b, side):
        acts = jnp.concatenate(
            [act_a[side * 64 : side * 64 + 64], act_b[side * 64 : side * 64 + 64]], axis=0
        )
        left = dot(acts, down[:, 0:HALF])
        right = dot(acts, down[:, HALF:])
        rows = slice(side * ROWS, side * ROWS + ROWS)
        first = jnp.concatenate(
            [left[0:64].reshape(8, 8, HALF), right[0:64].reshape(8, 8, HALF)], axis=1
        )
        part[u, rows, 0:HALF] = first.reshape(ROWS, HALF).astype(BF16)
        left_b, right_b = left[64:].reshape(8, 8, HALF), right[64:].reshape(8, 8, HALF)
        upper = lax.broadcasted_iota(jnp.int32, (8, 8, QUART), 1) < 4
        last = jnp.concatenate(
            [
                jnp.where(upper, left_b[:, :, :QUART], left_b[:, :, QUART:]),
                jnp.where(upper, right_b[:, :, :QUART], right_b[:, :, QUART:]),
            ],
            axis=1,
        )
        part[u, rows, HALF:] = last.reshape(ROWS, QUART).astype(BF16)

    def compute(u, between=()):
        between = list(between)

        def run(count):
            for _ in range(min(count, len(between))):
                between.pop(0)()

        for i in range(8):
            y_copy(u, i).wait_recv()
        act_a, act_b = hidden(u)
        run(3)
        project(u, act_a, act_b, 1)
        for i in range(8):
            s_copy(u, i).start()
        run(2)
        project(u, act_a, act_b, 0)
        run(len(between))

    def give_back(u, i):
        s_copy(u, i).wait_recv()
        rows = block(target(i))
        value = (part[u, rows].astype(F32) + yret[u, rows].astype(F32)).astype(BF16)
        if i == 7:
            back[u, rows] = value
        else:
            summed[u, rows] = value
            r_copy(u, i).start()

    def combine(u):
        for i in range(7):
            r_copy(u, i).wait_recv()
        first = dot(mix_a[u], back[u, :, 0:HALF])
        last = dot(mix_b[u], back[u, :, HALF:])
        for q in range(4):
            h, c = q // 2, (q % 2) * QUART
            mixed = (
                states[u, :, q * QUART : (q + 1) * QUART].astype(F32)
                + first[h * 64 : h * 64 + 32, c : c + QUART]
                + first[h * 64 + 32 : h * 64 + 64, c : c + QUART]
                + last[q * 64 : q * 64 + 32]
                + last[q * 64 + 32 : q * 64 + 64]
            )
            outs[u, :, q * QUART : (q + 1) * QUART] = mixed.astype(BF16)
        out_copy(u).start()

    def out_copy(u):
        return pltpu.make_async_copy(outs.at[u], out_hbm.at[0, u // 2, u % 2], out_sem.at[u])

    def sends(d):
        return sec < sections - 1 if d == 0 else sec > 0

    def takes(d):
        return sec > 0 if d == 0 else sec < sections - 1

    def shift(d):
        @pl.when(sends(d))
        def _():
            h_copy(d).start()

    def arrive(d):
        @pl.when(takes(d))
        def _():
            h_copy(d).wait_recv()

        @pl.when(jnp.logical_not(takes(d)))
        def _():
            (enter_up if d == 0 else enter_down).wait()

    def grad_local():
        turned = dense[...].T
        high, rest = split_two(turned)
        mid, low = split_two(turned - high.astype(F32))
        stacked = jnp.concatenate(
            [high.astype(F32), mid.astype(F32), low.astype(F32), jnp.zeros((8, 4 * TOK), F32)], axis=0
        ).astype(BF16)
        terms = dot(stacked, normed[...])
        gfull[:, 0:D] = terms[0:8] + terms[8:16] + terms[16:24]
        gfull[:, D:] = jnp.zeros((8, 128), F32)
        for p in range(16):
            piece = gfull[:, p * PART : p * PART + 256]
            gsend[p % 2, p // 2] = jnp.concatenate(
                [piece, jnp.zeros((8, 256), F32)], axis=0
            ).astype(BF16)
        g_copy(7).start()

    def grad_share():
        g_copy(7).wait_recv()
        gsum[...] = (gsend[dp].astype(F32) + grecv[...].astype(F32)).astype(BF16)
        for i in range(7):
            g_copy(i).start()
        gall[me] = gsum[me]

    def grad_total():
        for i in range(7):
            g_copy(i).wait_recv()
        grads[0] = jnp.sum(gall[...].astype(F32), axis=0)[0:8, 0:PART]

    fwd = [[functools.partial(forward, u, i) for i in range(7)] for u in range(UNITS)]
    ret = [[functools.partial(give_back, u, i) for i in range(8)] for u in range(UNITS)]

    slots(0)
    loads[0].wait()
    norm(0)
    pack(0)
    greeted = 8 + (sec > 0).astype(jnp.int32) + (sec < sections - 1).astype(jnp.int32)
    pl.semaphore_wait(barrier, greeted)
    dispatch(0)
    slots(1)
    loads[1].wait()
    norm(1)
    pack(1)
    dispatch(1)
    gate(0)
    gate(1)
    slots(2)
    slots(3)
    for step in fwd[0]:
        step()
    loads[2].wait()
    loads[3].wait()
    for tick in range(TICKS):
        a, b = 2 * tick, 2 * tick + 1
        compute(a, fwd[b])
        compute(b, ret[a][:5])
        for step in ret[a][5:]:
            step()
        for step in ret[b][:2]:
            step()
        combine(a)
        if tick + 1 < TICKS:
            shift(0)
        for step in ret[b][2:]:
            step()
        if tick + 1 < TICKS:
            arrive(0)
            norm(a + 2)
            pack(a + 2)
            dispatch(a + 2)
            gate(a + 2)
        combine(b)
        if tick + 1 < TICKS:
            shift(1)
            arrive(1)
            norm(b + 2)
            pack(b + 2)
            dispatch(b + 2)
            gate(b + 2)
            grad_local()
            for step in fwd[a + 2]:
                step()
            grad_share()
    grad_total()

    for u in range(UNITS):
        for i in range(7):
            z_copy(u, i).wait_send()
            r_copy(u, i).wait_send()
        for i in range(8):
            y_copy(u, i).wait_send()
            s_copy(u, i).wait_send()
        out_copy(u).wait()
    for i in range(8):
        g_copy(i).wait_send()
    for d in range(2):

        @pl.when(sends(d))
        def _():
            h_copy(d).wait_send()


def per_device(held, entering, gain, router, up, down, routes, cot):
    width = up.shape[-1]
    hbm = pl.BlockSpec(memory_space=pl.ANY)
    vmem = pl.BlockSpec(memory_space=pltpu.VMEM)
    dma = pltpu.SemaphoreType.DMA
    return pl.pallas_call(
        kernel,
        out_shape=(
            jax.ShapeDtypeStruct((1, TICKS, 2, TOK, D), BF16),
            jax.ShapeDtypeStruct((1, NE, PART), F32),
        ),
        in_specs=[hbm, hbm, vmem, vmem, hbm, hbm, vmem, vmem],
        out_specs=(hbm, vmem),
        scratch_shapes=[
            pltpu.VMEM((UNITS, TOK, D), BF16),
            pltpu.VMEM((UNITS * TOK, D), BF16),
            pltpu.VMEM((D, width), BF16),
            pltpu.VMEM((width, D), BF16),
            pltpu.VMEM((UNITS, ROWS, PACK), BF16),
            pltpu.VMEM((UNITS, 2 * ROWS, PACK), BF16),
            pltpu.VMEM((UNITS, 2 * ROWS, PACK), BF16),
            pltpu.VMEM((UNITS, ROWS, PACK), BF16),
            pltpu.VMEM((UNITS, ROWS, PACK), BF16),
            pltpu.VMEM((UNITS, ROWS, PACK), BF16),
            pltpu.VMEM((UNITS, TOK, D), BF16),
            pltpu.VMEM((UNITS, 192, ROWS), F32),
            pltpu.VMEM((UNITS, ROWS, 64), BF16),
            pltpu.VMEM((UNITS, ROWS, ROWS), BF16),
            pltpu.VMEM((UNITS, 128, ROWS), BF16),
            pltpu.VMEM((UNITS, 256, ROWS), BF16),
            pltpu.VMEM((UNITS * TOK, NE), F32),
            pltpu.VMEM((NE, D + 128), F32),
            pltpu.VMEM((2, NE, 16, 256), BF16),
            pltpu.VMEM((NE, 16, 256), BF16),
            pltpu.VMEM((NE, 16, 256), BF16),
            pltpu.VMEM((NE, 16, 256), BF16),
            dma((6,)),
            dma((UNITS,)),
            dma((UNITS, 7)),
            dma((UNITS, 7)),
            dma((UNITS, 8)),
            dma((UNITS, 8)),
            dma((UNITS, 8)),
            dma((UNITS, 8)),
            dma((UNITS, 7)),
            dma((UNITS, 7)),
            dma((2,)),
            dma((2,)),
            dma((8,)),
            dma((8,)),
        ],
        compiler_params=pltpu.CompilerParams(
            collective_id=0, has_side_effects=True, vmem_limit_bytes=56 << 20
        ),
        cost_estimate=pl.CostEstimate(
            flops=12_000_000_000, bytes_accessed=12_000_000, transcendentals=1_000_000
        ),
    )(held, entering, gain, router, up, down, routes, cot)


def solution(mesh):
    placed = (
        P("section", None, ("expert", "dp"), None),
        P(None, None, ("expert", "dp"), None),
        P("section", None),
        P("section", None, None),
        P("section", "expert", None, "dp"),
        P("section", "expert", "dp", None),
        P("section", None, None, "expert", None),
        P("section", None, None, ("expert", "dp"), None),
    )
    return jax.shard_map(
        per_device,
        mesh=mesh,
        in_specs=placed,
        out_specs=(
            P("section", None, None, ("expert", "dp"), None),
            P("section", None, ("expert", "dp")),
        ),
        check_vma=False,
    )
```

```python
import functools

import jax
import jax.numpy as jnp
from jax import lax
from jax.experimental import pallas as pl
from jax.experimental.pallas import tpu as pltpu
from jax.sharding import PartitionSpec as P

TICKS = 2
UNITS = 4
D = 3584
TOK = 32
NE = 8
HALF = D // 2
QUART = D // 4
PACK = HALF + QUART
ROWS = NE * 16
PART = D // 16
SCALE = 2.5
MESH = pl.DeviceIdType.MESH
F32 = jnp.float32
BF16 = jnp.bfloat16
RING = (1, 7, 2, 6, 3, 5, 4)
BACK = (4, 3, 5, 2, 6, 1, 7)


def dot(a, b):
    return jnp.dot(a, b, preferred_element_type=F32)


def split_two(value):
    high = value.astype(BF16)
    return high, (value - high.astype(F32)).astype(BF16)


def kernel(
    held,
    entering,
    gain,
    router,
    up_hbm,
    down_hbm,
    routes,
    cot,
    out_hbm,
    grads,
    states,
    normed,
    up,
    down,
    packed,
    gath,
    part,
    yret,
    summed,
    back,
    outs,
    place,
    place_a,
    place_b,
    mix_a,
    mix_b,
    route_rows,
    cot_rows,
    dense,
    gfull,
    gsend,
    grecv,
    gsum,
    gall,
    in_sem,
    out_sem,
    zs,
    zr,
    ys,
    yr,
    ss,
    sr,
    rs,
    rr,
    hs,
    hr,
    gs,
    gr,
):
    sec = lax.axis_index("section")
    me = lax.axis_index("expert")
    dp = lax.axis_index("dp")
    sections = lax.axis_size("section")

    def ring(offset):
        return lax.rem(me + offset + NE, NE)

    def block(index):
        return pl.ds(pl.multiple_of(index * 16, 16), 16)

    def other(index):
        return pl.ds(pl.multiple_of(index * 16 + ROWS, 16), 16)

    barrier = pltpu.get_barrier_semaphore()
    for offset in RING:
        pl.semaphore_signal(barrier, inc=1, device_id={"expert": ring(offset)}, device_id_type=MESH)
    pl.semaphore_signal(barrier, inc=1, device_id={"dp": 1 - dp}, device_id_type=MESH)

    @pl.when(sec > 0)
    def _():
        pl.semaphore_signal(barrier, inc=1, device_id={"section": sec - 1}, device_id_type=MESH)

    @pl.when(sec < sections - 1)
    def _():
        pl.semaphore_signal(barrier, inc=1, device_id={"section": sec + 1}, device_id_type=MESH)

    loads = [
        pltpu.make_async_copy(held.at[0, 0], states.at[0], in_sem.at[0]),
        pltpu.make_async_copy(held.at[0, 1], states.at[1], in_sem.at[1]),
        pltpu.make_async_copy(up_hbm.at[0, 0], up, in_sem.at[2]),
        pltpu.make_async_copy(down_hbm.at[0, 0], down, in_sem.at[3]),
    ]
    for load in loads:
        load.start()
    enter_up = pltpu.make_async_copy(entering.at[0, 0], states.at[2], in_sem.at[4])
    enter_down = pltpu.make_async_copy(entering.at[0, 1], states.at[3], in_sem.at[5])

    @pl.when(sec == 0)
    def _():
        enter_up.start()

    @pl.when(sec == sections - 1)
    def _():
        enter_down.start()

    def z_copy(u, i):
        to = ring(RING[i])
        return pltpu.make_async_remote_copy(
            src_ref=packed.at[u, block(to)],
            dst_ref=gath.at[u, block(me)],
            send_sem=zs.at[u, i],
            recv_sem=zr.at[u, i],
            device_id={"expert": to},
            device_id_type=MESH,
        )

    def origin(i):
        return me if i == 7 else ring(-RING[i])

    def y_copy(u, i):
        src = packed if i == 7 else gath
        return pltpu.make_async_remote_copy(
            src_ref=src.at[u, block(origin(i))],
            dst_ref=gath.at[u, other(origin(i))],
            send_sem=ys.at[u, i],
            recv_sem=yr.at[u, i],
            device_id={"dp": 1 - dp},
            device_id_type=MESH,
        )

    def target(i):
        return me if i == 7 else ring(BACK[i])

    def s_copy(u, i):
        return pltpu.make_async_remote_copy(
            src_ref=part.at[u, other(target(i))],
            dst_ref=yret.at[u, block(target(i))],
            send_sem=ss.at[u, i],
            recv_sem=sr.at[u, i],
            device_id={"dp": 1 - dp},
            device_id_type=MESH,
        )

    def r_copy(u, i):
        to = ring(BACK[i])
        return pltpu.make_async_remote_copy(
            src_ref=summed.at[u, block(to)],
            dst_ref=back.at[u, block(me)],
            send_sem=rs.at[u, i],
            recv_sem=rr.at[u, i],
            device_id={"expert": to},
            device_id_type=MESH,
        )

    def h_copy(d):
        return pltpu.make_async_remote_copy(
            src_ref=outs.at[d],
            dst_ref=states.at[2 + d],
            send_sem=hs.at[d],
            recv_sem=hr.at[d],
            device_id={"section": sec + 1 if d == 0 else sec - 1},
            device_id_type=MESH,
        )

    def g_copy(i):
        if i == 7:
            return pltpu.make_async_remote_copy(
                src_ref=gsend.at[1 - dp],
                dst_ref=grecv,
                send_sem=gs.at[7],
                recv_sem=gr.at[7],
                device_id={"dp": 1 - dp},
                device_id_type=MESH,
            )
        to = ring(RING[i])
        return pltpu.make_async_remote_copy(
            src_ref=gsum.at[to],
            dst_ref=gall.at[me],
            send_sem=gs.at[i],
            recv_sem=gr.at[i],
            device_id={"expert": to},
            device_id_type=MESH,
        )

    def rows_of(u):
        return slice(u * TOK, (u + 1) * TOK)

    def turn():
        pairs = [(t, d) for t in range(TICKS) for d in range(2)]
        named = jnp.concatenate([routes[0, t, d] for t, d in pairs], axis=0)
        route_rows[...] = named.astype(F32).T.astype(jnp.int32)
        cot_rows[...] = jnp.concatenate([cot[0, t, d] for t, d in pairs], axis=0).T

    def own_routes(u):
        return route_rows[pl.ds(pl.multiple_of(dp * TOK, TOK), TOK), 2 * u : 2 * u + 2]

    def slots(u):
        chosen = own_routes(u)
        lane = lax.broadcasted_iota(jnp.int32, (TOK, ROWS), 1)
        expert, row = lane // 16, lane % 16
        hit = (chosen[:, 0:1] == expert) | (chosen[:, 1:2] == expert)
        earlier = lax.broadcasted_iota(jnp.int32, (TOK, TOK), 0) > lax.broadcasted_iota(
            jnp.int32, (TOK, TOK), 1
        )
        rank = dot(earlier.astype(F32).astype(BF16), hit.astype(F32).astype(BF16)).astype(jnp.int32)
        first = hit & (rank == row % 8)
        last = hit & (rank == 8 + row % 4)
        pa = jnp.concatenate([(first & (row // 8 == h)).astype(F32) for h in range(2)], axis=0)
        pb = jnp.concatenate([(last & (row // 4 == q)).astype(F32) for q in range(4)], axis=0)
        place[u, 0:64] = pa
        place[u, 64:192] = pb
        place_a[u] = pa.T.astype(BF16)
        place_b[u] = pb.T.astype(BF16)

    def norm(u):
        values = states[u].astype(F32)
        meansq = jnp.mean(values * values, axis=-1, keepdims=True)
        normed[rows_of(u)] = (
            values * lax.rsqrt(meansq + 1e-06) * gain[...].astype(F32)
        ).astype(BF16)

    def pack(u):
        own = normed[rows_of(u)]
        halves = jnp.concatenate([own[:, :HALF], own[:, HALF:]], axis=0)
        packed[u, :, 0:HALF] = dot(place_a[u], halves).astype(BF16)
        quarters = jnp.concatenate([own[:, q * QUART : (q + 1) * QUART] for q in range(4)], axis=0)
        packed[u, :, HALF:] = dot(place_b[u], quarters).astype(BF16)

    def dispatch(u):
        for i in range(7):
            z_copy(u, i).start()
        y_copy(u, 7).start()
        gath[u, block(me)] = packed[u, block(me)]

    def forward(u, i):
        z_copy(u, i).wait_recv()
        y_copy(u, i).start()

    def gate(u):
        chosen = own_routes(u)
        cotangent = cot_rows[:, 2 * u : 2 * u + 2]
        logits = lax.dot_general(
            normed[rows_of(u)], router[0], (((1,), (1,)), ((), ())), preferred_element_type=F32
        )
        lane = lax.broadcasted_iota(jnp.int32, (TOK, NE), 1)
        hit0, hit1 = chosen[:, 0:1] == lane, chosen[:, 1:2] == lane
        affinity = jnp.where(hit0 | hit1, jax.nn.sigmoid(logits), 0.0)
        total = jnp.sum(affinity, axis=1, keepdims=True)
        weights = SCALE * affinity / total
        cots = jnp.where(hit0, cotangent[:, 0:1], 0.0) + jnp.where(hit1, cotangent[:, 1:2], 0.0)
        inner = jnp.sum(cots * affinity, axis=1, keepdims=True)
        slope = SCALE * (cots / total - inner / (total * total))
        dense[rows_of(u)] = slope * affinity * (1.0 - affinity)
        expert = lax.broadcasted_iota(jnp.int32, (TOK, ROWS), 1) // 16
        spread = jnp.zeros((TOK, ROWS), F32)
        for e in range(NE):
            spread = jnp.where(expert == e, weights[:, e : e + 1], spread)
        high, low = split_two(spread)
        high, low = high.astype(F32), low.astype(F32)
        for h in range(6):
            hot = place[u, h * TOK : (h + 1) * TOK]
            both = jnp.concatenate([hot * high, hot * low], axis=0).astype(BF16)
            if h < 2:
                mix_a[u, h * 64 : (h + 1) * 64] = both
            else:
                mix_b[u, (h - 2) * 64 : (h - 1) * 64] = both

    def hidden(u):
        first = gath[u, :, 0:HALF]
        left = dot(first, up[0:HALF]).reshape(16, 2, 8, 512)
        right = dot(first, up[HALF:]).reshape(16, 2, 8, 512)
        pre_a = (left[:, 0] + right[:, 1]).reshape(128, 512)
        last = gath[u, :, HALF:]
        upper = lax.broadcasted_iota(jnp.int32, (16, 8, 512), 1) < 4
        quart = [
            dot(last, up[g * QUART : (g + 1) * QUART]).reshape(16, 2, 8, 512)[:, g // 2]
            for g in range(4)
        ]
        halves = jnp.where(upper, quart[0] + quart[2], quart[1] + quart[3])
        pre_b = (halves + pltpu.roll(halves, 4, 1)).reshape(128, 512)
        act_a = (pre_a * jax.nn.sigmoid(pre_a)).astype(BF16)
        act_b = (pre_b * jax.nn.sigmoid(pre_b)).astype(BF16)
        return act_a, act_b

    def project(u, act_a, act_b, side):
        acts = jnp.concatenate(
            [act_a[side * 64 : side * 64 + 64], act_b[side * 64 : side * 64 + 64]], axis=0
        )
        left = dot(acts, down[:, 0:HALF])
        right = dot(acts, down[:, HALF:])
        rows = slice(side * ROWS, side * ROWS + ROWS)
        first = jnp.concatenate(
            [left[0:64].reshape(8, 8, HALF), right[0:64].reshape(8, 8, HALF)], axis=1
        )
        part[u, rows, 0:HALF] = first.reshape(ROWS, HALF).astype(BF16)
        left_b, right_b = left[64:].reshape(8, 8, HALF), right[64:].reshape(8, 8, HALF)
        upper = lax.broadcasted_iota(jnp.int32, (8, 8, QUART), 1) < 4
        last = jnp.concatenate(
            [
                jnp.where(upper, left_b[:, :, :QUART], left_b[:, :, QUART:]),
                jnp.where(upper, right_b[:, :, :QUART], right_b[:, :, QUART:]),
            ],
            axis=1,
        )
        part[u, rows, HALF:] = last.reshape(ROWS, QUART).astype(BF16)

    def compute(u, between=()):
        between = list(between)

        def run(count):
            for _ in range(min(count, len(between))):
                between.pop(0)()

        for i in range(8):
            y_copy(u, i).wait_recv()
        act_a, act_b = hidden(u)
        run(3)
        project(u, act_a, act_b, 1)
        for i in range(8):
            s_copy(u, i).start()
        run(2)
        project(u, act_a, act_b, 0)
        run(len(between))

    def give_back(u, i):
        s_copy(u, i).wait_recv()
        rows = block(target(i))
        value = (part[u, rows].astype(F32) + yret[u, rows].astype(F32)).astype(BF16)
        if i == 7:
            back[u, rows] = value
        else:
            summed[u, rows] = value
            r_copy(u, i).start()

    def combine(u):
        for i in range(7):
            r_copy(u, i).wait_recv()
        first = dot(mix_a[u], back[u, :, 0:HALF])
        last = dot(mix_b[u], back[u, :, HALF:])
        for q in range(4):
            h, c = q // 2, (q % 2) * QUART
            mixed = (
                states[u, :, q * QUART : (q + 1) * QUART].astype(F32)
                + first[h * 64 : h * 64 + 32, c : c + QUART]
                + first[h * 64 + 32 : h * 64 + 64, c : c + QUART]
                + last[q * 64 : q * 64 + 32]
                + last[q * 64 + 32 : q * 64 + 64]
            )
            outs[u, :, q * QUART : (q + 1) * QUART] = mixed.astype(BF16)
        out_copy(u).start()

    def out_copy(u):
        return pltpu.make_async_copy(outs.at[u], out_hbm.at[0, u // 2, u % 2], out_sem.at[u])

    def sends(d):
        return sec < sections - 1 if d == 0 else sec > 0

    def takes(d):
        return sec > 0 if d == 0 else sec < sections - 1

    def shift(d):
        @pl.when(sends(d))
        def _():
            h_copy(d).start()

    def arrive(d):
        @pl.when(takes(d))
        def _():
            h_copy(d).wait_recv()

        @pl.when(jnp.logical_not(takes(d)))
        def _():
            (enter_up if d == 0 else enter_down).wait()

    def grad_local():
        turned = dense[...].T
        high, rest = split_two(turned)
        mid, low = split_two(turned - high.astype(F32))
        stacked = jnp.concatenate(
            [high.astype(F32), mid.astype(F32), low.astype(F32), jnp.zeros((8, 4 * TOK), F32)], axis=0
        ).astype(BF16)
        terms = dot(stacked, normed[...])
        gfull[:, 0:D] = terms[0:8] + terms[8:16] + terms[16:24]
        gfull[:, D:] = jnp.zeros((8, 128), F32)
        for p in range(16):
            piece = gfull[:, p * PART : p * PART + 256]
            gsend[p % 2, p // 2] = jnp.concatenate(
                [piece, jnp.zeros((8, 256), F32)], axis=0
            ).astype(BF16)
        g_copy(7).start()

    def grad_share():
        g_copy(7).wait_recv()
        gsum[...] = (gsend[dp].astype(F32) + grecv[...].astype(F32)).astype(BF16)
        for i in range(7):
            g_copy(i).start()
        gall[me] = gsum[me]

    def grad_total():
        for i in range(7):
            g_copy(i).wait_recv()
        grads[0] = jnp.sum(gall[...].astype(F32), axis=0)[0:8, 0:PART]

    turn()
    slots(0)
    loads[0].wait()
    norm(0)
    pack(0)
    pl.semaphore_wait(barrier, 8 + (sec > 0).astype(jnp.int32) + (sec < sections - 1).astype(jnp.int32))
    z_copy(0, 0).start()
    z_copy(0, 1).start()
    z_copy(0, 2).start()
    z_copy(0, 3).start()
    z_copy(0, 4).start()
    z_copy(0, 5).start()
    z_copy(0, 6).start()
    y_copy(0, 7).start()
    gath[0, block(me)] = packed[0, block(me)]
    slots(1)
    loads[1].wait()
    norm(1)
    pack(1)
    z_copy(1, 0).start()
    z_copy(1, 1).start()
    z_copy(1, 2).start()
    z_copy(1, 3).start()
    z_copy(1, 4).start()
    z_copy(1, 5).start()
    z_copy(1, 6).start()
    y_copy(1, 7).start()
    gath[1, block(me)] = packed[1, block(me)]
    gate(0)
    gate(1)
    forward(0, 0)
    forward(0, 1)
    forward(0, 2)
    forward(0, 3)
    forward(0, 4)
    forward(0, 5)
    forward(0, 6)
    loads[2].wait()
    loads[3].wait()
    slots(2)
    slots(3)
    forward(1, 0)
    forward(1, 1)
    for i in range(8):
        y_copy(0, i).wait_recv()
    hid0 = hidden(0)
    project(0, *hid0, 1)
    for i in range(8):
        s_copy(0, i).start()
    forward(1, 2)
    forward(1, 3)
    project(0, *hid0, 0)
    forward(1, 4)
    give_back(0, 0)
    forward(1, 5)
    give_back(0, 1)
    forward(1, 6)
    give_back(0, 2)
    give_back(0, 3)
    for i in range(8):
        y_copy(1, i).wait_recv()
    hid1 = hidden(1)
    project(1, *hid1, 1)
    for i in range(8):
        s_copy(1, i).start()
    give_back(0, 4)
    give_back(0, 5)
    project(1, *hid1, 0)
    give_back(0, 6)
    give_back(0, 7)
    give_back(1, 0)
    give_back(1, 1)
    combine(0)
    shift(0)
    give_back(1, 2)
    give_back(1, 3)
    arrive(0)
    norm(2)
    pack(2)
    z_copy(2, 0).start()
    z_copy(2, 1).start()
    z_copy(2, 2).start()
    z_copy(2, 3).start()
    z_copy(2, 4).start()
    z_copy(2, 5).start()
    z_copy(2, 6).start()
    y_copy(2, 7).start()
    gath[2, block(me)] = packed[2, block(me)]
    gate(2)
    give_back(1, 4)
    forward(2, 0)
    give_back(1, 5)
    forward(2, 1)
    give_back(1, 6)
    forward(2, 2)
    give_back(1, 7)
    forward(2, 3)
    combine(1)
    shift(1)
    forward(2, 4)
    arrive(1)
    norm(3)
    pack(3)
    z_copy(3, 0).start()
    z_copy(3, 1).start()
    z_copy(3, 2).start()
    z_copy(3, 3).start()
    z_copy(3, 4).start()
    z_copy(3, 5).start()
    z_copy(3, 6).start()
    y_copy(3, 7).start()
    gath[3, block(me)] = packed[3, block(me)]
    forward(2, 5)
    forward(2, 6)
    gate(3)
    grad_local()
    grad_share()
    forward(3, 0)
    forward(3, 1)
    for i in range(8):
        y_copy(2, i).wait_recv()
    hid2 = hidden(2)
    project(2, *hid2, 1)
    for i in range(8):
        s_copy(2, i).start()
    forward(3, 2)
    forward(3, 3)
    project(2, *hid2, 0)
    forward(3, 4)
    give_back(2, 0)
    forward(3, 5)
    give_back(2, 1)
    forward(3, 6)
    give_back(2, 2)
    give_back(2, 3)
    for i in range(8):
        y_copy(3, i).wait_recv()
    hid3 = hidden(3)
    project(3, *hid3, 1)
    for i in range(8):
        s_copy(3, i).start()
    give_back(2, 4)
    give_back(2, 5)
    project(3, *hid3, 0)
    give_back(2, 6)
    give_back(2, 7)
    give_back(3, 0)
    give_back(3, 1)
    combine(2)
    give_back(3, 2)
    give_back(3, 3)
    give_back(3, 4)
    give_back(3, 5)
    give_back(3, 6)
    give_back(3, 7)
    grad_total()
    combine(3)

    for u in range(UNITS):
        for i in range(7):
            z_copy(u, i).wait_send()
            r_copy(u, i).wait_send()
        for i in range(8):
            y_copy(u, i).wait_send()
            s_copy(u, i).wait_send()
        out_copy(u).wait()
    for i in range(8):
        g_copy(i).wait_send()
    for d in range(2):

        @pl.when(sends(d))
        def _():
            h_copy(d).wait_send()


def per_device(held, entering, gain, router, up, down, routes, cot):
    width = up.shape[-1]
    hbm = pl.BlockSpec(memory_space=pl.ANY)
    vmem = pl.BlockSpec(memory_space=pltpu.VMEM)
    dma = pltpu.SemaphoreType.DMA
    return pl.pallas_call(
        kernel,
        out_shape=(
            jax.ShapeDtypeStruct((1, TICKS, 2, TOK, D), BF16),
            jax.ShapeDtypeStruct((1, NE, PART), F32),
        ),
        in_specs=[hbm, hbm, vmem, vmem, hbm, hbm, vmem, vmem],
        out_specs=(hbm, vmem),
        scratch_shapes=[
            pltpu.VMEM((UNITS, TOK, D), BF16),
            pltpu.VMEM((UNITS * TOK, D), BF16),
            pltpu.VMEM((D, width), BF16),
            pltpu.VMEM((width, D), BF16),
            pltpu.VMEM((UNITS, ROWS, PACK), BF16),
            pltpu.VMEM((UNITS, 2 * ROWS, PACK), BF16),
            pltpu.VMEM((UNITS, 2 * ROWS, PACK), BF16),
            pltpu.VMEM((UNITS, ROWS, PACK), BF16),
            pltpu.VMEM((UNITS, ROWS, PACK), BF16),
            pltpu.VMEM((UNITS, ROWS, PACK), BF16),
            pltpu.VMEM((UNITS, TOK, D), BF16),
            pltpu.VMEM((UNITS, 192, ROWS), F32),
            pltpu.VMEM((UNITS, ROWS, 64), BF16),
            pltpu.VMEM((UNITS, ROWS, ROWS), BF16),
            pltpu.VMEM((UNITS, 128, ROWS), BF16),
            pltpu.VMEM((UNITS, 256, ROWS), BF16),
            pltpu.VMEM((2 * TOK, 2 * UNITS), jnp.int32),
            pltpu.VMEM((TOK, 2 * UNITS), F32),
            pltpu.VMEM((UNITS * TOK, NE), F32),
            pltpu.VMEM((NE, D + 128), F32),
            pltpu.VMEM((2, NE, 16, 256), BF16),
            pltpu.VMEM((NE, 16, 256), BF16),
            pltpu.VMEM((NE, 16, 256), BF16),
            pltpu.VMEM((NE, 16, 256), BF16),
            dma((6,)),
            dma((UNITS,)),
            dma((UNITS, 7)),
            dma((UNITS, 7)),
            dma((UNITS, 8)),
            dma((UNITS, 8)),
            dma((UNITS, 8)),
            dma((UNITS, 8)),
            dma((UNITS, 7)),
            dma((UNITS, 7)),
            dma((2,)),
            dma((2,)),
            dma((8,)),
            dma((8,)),
        ],
        compiler_params=pltpu.CompilerParams(
            collective_id=0, has_side_effects=True, vmem_limit_bytes=56 << 20
        ),
        cost_estimate=pl.CostEstimate(
            flops=12_000_000_000, bytes_accessed=12_000_000, transcendentals=1_000_000
        ),
    )(held, entering, gain, router, up, down, jnp.swapaxes(routes, 3, 4), jnp.swapaxes(cot, 3, 4))


def solution(mesh):
    placed = (
        P("section", None, ("expert", "dp"), None),
        P(None, None, ("expert", "dp"), None),
        P("section", None),
        P("section", None, None),
        P("section", "expert", None, "dp"),
        P("section", "expert", "dp", None),
        P("section", None, None, "expert", None),
        P("section", None, None, ("expert", "dp"), None),
    )
    return jax.shard_map(
        per_device,
        mesh=mesh,
        in_specs=placed,
        out_specs=(
            P("section", None, None, ("expert", "dp"), None),
            P("section", None, ("expert", "dp")),
        ),
        check_vma=False,
    )
```

```python
import functools

import jax
import jax.numpy as jnp
from jax import lax
from jax.experimental import pallas as pl
from jax.experimental.pallas import tpu as pltpu
from jax.sharding import PartitionSpec as P

TICKS = 2
UNITS = 4
D = 3584
TOK = 32
NE = 8
HALF = D // 2
QUART = D // 4
PACK = HALF + QUART
ROWS = NE * 16
PART = D // 16
SCALE = 2.5
MESH = pl.DeviceIdType.MESH
F32 = jnp.float32
BF16 = jnp.bfloat16
RING = (1, 7, 2, 6, 3, 5, 4)
BACK = (4, 3, 5, 2, 6, 1, 7)


def dot(a, b):
    return jnp.dot(a, b, preferred_element_type=F32)


def split_two(value):
    high = value.astype(BF16)
    return high, (value - high.astype(F32)).astype(BF16)


def kernel(
    held,
    entering,
    gain,
    router,
    up_hbm,
    down_hbm,
    routes,
    cot,
    out_hbm,
    grads,
    states,
    normed,
    up,
    down,
    packed,
    gath,
    part,
    yret,
    summed,
    back,
    outs,
    place,
    place_a,
    place_b,
    mix_a,
    mix_b,
    route_rows,
    cot_rows,
    dense,
    gfull,
    gsend,
    grecv,
    gsum,
    gall,
    in_sem,
    out_sem,
    zs,
    zr,
    ys,
    yr,
    ss,
    sr,
    rs,
    rr,
    hs,
    hr,
    gs,
    gr,
):
    sec = lax.axis_index("section")
    me = lax.axis_index("expert")
    dp = lax.axis_index("dp")
    sections = lax.axis_size("section")

    def ring(offset):
        return lax.rem(me + offset + NE, NE)

    def block(index):
        return pl.ds(pl.multiple_of(index * 16, 16), 16)

    def other(index):
        return pl.ds(pl.multiple_of(index * 16 + ROWS, 16), 16)

    barrier = pltpu.get_barrier_semaphore()
    for offset in RING:
        pl.semaphore_signal(barrier, inc=1, device_id={"expert": ring(offset)}, device_id_type=MESH)
    pl.semaphore_signal(barrier, inc=1, device_id={"dp": 1 - dp}, device_id_type=MESH)

    @pl.when(sec > 0)
    def _():
        pl.semaphore_signal(barrier, inc=1, device_id={"section": sec - 1}, device_id_type=MESH)

    @pl.when(sec < sections - 1)
    def _():
        pl.semaphore_signal(barrier, inc=1, device_id={"section": sec + 1}, device_id_type=MESH)

    loads = [
        pltpu.make_async_copy(held.at[0, 0], states.at[0], in_sem.at[0]),
        pltpu.make_async_copy(held.at[0, 1], states.at[1], in_sem.at[1]),
        pltpu.make_async_copy(up_hbm.at[0, 0], up, in_sem.at[2]),
        pltpu.make_async_copy(down_hbm.at[0, 0], down, in_sem.at[3]),
    ]
    for load in loads:
        load.start()
    enter_up = pltpu.make_async_copy(entering.at[0, 0], states.at[2], in_sem.at[4])
    enter_down = pltpu.make_async_copy(entering.at[0, 1], states.at[3], in_sem.at[5])

    @pl.when(sec == 0)
    def _():
        enter_up.start()

    @pl.when(sec == sections - 1)
    def _():
        enter_down.start()

    def z_copy(u, i):
        to = ring(RING[i])
        return pltpu.make_async_remote_copy(
            src_ref=packed.at[u, block(to)],
            dst_ref=gath.at[u, block(me)],
            send_sem=zs.at[u, i],
            recv_sem=zr.at[u, i],
            device_id={"expert": to},
            device_id_type=MESH,
        )

    def origin(i):
        return me if i == 7 else ring(-RING[i])

    def y_copy(u, i):
        src = packed if i == 7 else gath
        return pltpu.make_async_remote_copy(
            src_ref=src.at[u, block(origin(i))],
            dst_ref=gath.at[u, other(origin(i))],
            send_sem=ys.at[u, i],
            recv_sem=yr.at[u, i],
            device_id={"dp": 1 - dp},
            device_id_type=MESH,
        )

    def target(i):
        return me if i == 7 else ring(BACK[i])

    def s_copy(u, i):
        return pltpu.make_async_remote_copy(
            src_ref=part.at[u, other(target(i))],
            dst_ref=yret.at[u, block(target(i))],
            send_sem=ss.at[u, i],
            recv_sem=sr.at[u, i],
            device_id={"dp": 1 - dp},
            device_id_type=MESH,
        )

    def r_copy(u, i):
        to = ring(BACK[i])
        return pltpu.make_async_remote_copy(
            src_ref=summed.at[u, block(to)],
            dst_ref=back.at[u, block(me)],
            send_sem=rs.at[u, i],
            recv_sem=rr.at[u, i],
            device_id={"expert": to},
            device_id_type=MESH,
        )

    def h_copy(d):
        return pltpu.make_async_remote_copy(
            src_ref=outs.at[d],
            dst_ref=states.at[2 + d],
            send_sem=hs.at[d],
            recv_sem=hr.at[d],
            device_id={"section": sec + 1 if d == 0 else sec - 1},
            device_id_type=MESH,
        )

    def g_copy(i):
        if i == 7:
            return pltpu.make_async_remote_copy(
                src_ref=gsend.at[1 - dp],
                dst_ref=grecv,
                send_sem=gs.at[7],
                recv_sem=gr.at[7],
                device_id={"dp": 1 - dp},
                device_id_type=MESH,
            )
        to = ring(RING[i])
        return pltpu.make_async_remote_copy(
            src_ref=gsum.at[to],
            dst_ref=gall.at[me],
            send_sem=gs.at[i],
            recv_sem=gr.at[i],
            device_id={"expert": to},
            device_id_type=MESH,
        )

    def rows_of(u):
        return slice(u * TOK, (u + 1) * TOK)

    def turn():
        pairs = [(t, d) for t in range(TICKS) for d in range(2)]
        named = jnp.concatenate([routes[0, t, d] for t, d in pairs], axis=0)
        route_rows[...] = named.astype(F32).T.astype(jnp.int32)
        cot_rows[...] = jnp.concatenate([cot[0, t, d] for t, d in pairs], axis=0).T

    def own_routes(u):
        return route_rows[pl.ds(pl.multiple_of(dp * TOK, TOK), TOK), 2 * u : 2 * u + 2]

    def slots(u):
        chosen = own_routes(u)
        lane = lax.broadcasted_iota(jnp.int32, (TOK, ROWS), 1)
        expert, row = lane // 16, lane % 16
        hit = (chosen[:, 0:1] == expert) | (chosen[:, 1:2] == expert)
        earlier = lax.broadcasted_iota(jnp.int32, (TOK, TOK), 0) > lax.broadcasted_iota(
            jnp.int32, (TOK, TOK), 1
        )
        rank = dot(earlier.astype(F32).astype(BF16), hit.astype(F32).astype(BF16)).astype(jnp.int32)
        first = hit & (rank == row % 8)
        last = hit & (rank == 8 + row % 4)
        pa = jnp.concatenate([(first & (row // 8 == h)).astype(F32) for h in range(2)], axis=0)
        pb = jnp.concatenate([(last & (row // 4 == q)).astype(F32) for q in range(4)], axis=0)
        place[u, 0:64] = pa
        place[u, 64:192] = pb
        place_a[u] = pa.T.astype(BF16)
        place_b[u] = pb.T.astype(BF16)

    def norm(u):
        values = states[u].astype(F32)
        meansq = jnp.mean(values * values, axis=-1, keepdims=True)
        normed[rows_of(u)] = (
            values * lax.rsqrt(meansq + 1e-06) * gain[...].astype(F32)
        ).astype(BF16)

    def pack(u):
        own = normed[rows_of(u)]
        halves = jnp.concatenate([own[:, :HALF], own[:, HALF:]], axis=0)
        packed[u, :, 0:HALF] = dot(place_a[u], halves).astype(BF16)
        quarters = jnp.concatenate([own[:, q * QUART : (q + 1) * QUART] for q in range(4)], axis=0)
        packed[u, :, HALF:] = dot(place_b[u], quarters).astype(BF16)

    def dispatch(u):
        for i in range(7):
            z_copy(u, i).start()
        y_copy(u, 7).start()
        gath[u, block(me)] = packed[u, block(me)]

    def forward(u, i):
        z_copy(u, i).wait_recv()
        y_copy(u, i).start()

    def gate(u):
        chosen = own_routes(u)
        cotangent = cot_rows[:, 2 * u : 2 * u + 2]
        logits = lax.dot_general(
            normed[rows_of(u)], router[0], (((1,), (1,)), ((), ())), preferred_element_type=F32
        )
        lane = lax.broadcasted_iota(jnp.int32, (TOK, NE), 1)
        hit0, hit1 = chosen[:, 0:1] == lane, chosen[:, 1:2] == lane
        affinity = jnp.where(hit0 | hit1, jax.nn.sigmoid(logits), 0.0)
        total = jnp.sum(affinity, axis=1, keepdims=True)
        weights = SCALE * affinity / total
        cots = jnp.where(hit0, cotangent[:, 0:1], 0.0) + jnp.where(hit1, cotangent[:, 1:2], 0.0)
        inner = jnp.sum(cots * affinity, axis=1, keepdims=True)
        slope = SCALE * (cots / total - inner / (total * total))
        dense[rows_of(u)] = slope * affinity * (1.0 - affinity)
        expert = lax.broadcasted_iota(jnp.int32, (TOK, ROWS), 1) // 16
        spread = jnp.zeros((TOK, ROWS), F32)
        for e in range(NE):
            spread = jnp.where(expert == e, weights[:, e : e + 1], spread)
        high, low = split_two(spread)
        high, low = high.astype(F32), low.astype(F32)
        for h in range(6):
            hot = place[u, h * TOK : (h + 1) * TOK]
            both = jnp.concatenate([hot * high, hot * low], axis=0).astype(BF16)
            if h < 2:
                mix_a[u, h * 64 : (h + 1) * 64] = both
            else:
                mix_b[u, (h - 2) * 64 : (h - 1) * 64] = both

    def hidden(u, side):
        rows = slice(side * ROWS, side * ROWS + ROWS)
        first = gath[u, rows, 0:HALF]
        left = dot(first, up[0:HALF]).reshape(8, 2, 8, 512)
        right = dot(first, up[HALF:]).reshape(8, 2, 8, 512)
        pre_a = (left[:, 0] + right[:, 1]).reshape(64, 512)
        last = gath[u, rows, HALF:]
        upper = lax.broadcasted_iota(jnp.int32, (8, 8, 512), 1) < 4
        quart = [
            dot(last, up[g * QUART : (g + 1) * QUART]).reshape(8, 2, 8, 512)[:, g // 2]
            for g in range(4)
        ]
        halves = jnp.where(upper, quart[0] + quart[2], quart[1] + quart[3])
        pre_b = (halves + pltpu.roll(halves, 4, 1)).reshape(64, 512)
        pre = jnp.concatenate([pre_a, pre_b], axis=0)
        return (pre * jax.nn.sigmoid(pre)).astype(BF16)

    def project(u, acts, side):
        left = dot(acts, down[:, 0:HALF])
        right = dot(acts, down[:, HALF:])
        rows = slice(side * ROWS, side * ROWS + ROWS)
        first = jnp.concatenate(
            [left[0:64].reshape(8, 8, HALF), right[0:64].reshape(8, 8, HALF)], axis=1
        )
        part[u, rows, 0:HALF] = first.reshape(ROWS, HALF).astype(BF16)
        left_b, right_b = left[64:].reshape(8, 8, HALF), right[64:].reshape(8, 8, HALF)
        upper = lax.broadcasted_iota(jnp.int32, (8, 8, QUART), 1) < 4
        last = jnp.concatenate(
            [
                jnp.where(upper, left_b[:, :, :QUART], left_b[:, :, QUART:]),
                jnp.where(upper, right_b[:, :, :QUART], right_b[:, :, QUART:]),
            ],
            axis=1,
        )
        part[u, rows, HALF:] = last.reshape(ROWS, QUART).astype(BF16)

    def compute_own(u):
        project(u, hidden(u, 0), 0)

    def compute_other(u):
        for i in range(8):
            y_copy(u, i).wait_recv()
        project(u, hidden(u, 1), 1)

    def give_back(u, i):
        s_copy(u, i).wait_recv()
        rows = block(target(i))
        value = (part[u, rows].astype(F32) + yret[u, rows].astype(F32)).astype(BF16)
        if i == 7:
            back[u, rows] = value
        else:
            summed[u, rows] = value
            r_copy(u, i).start()

    def combine(u):
        for i in range(7):
            r_copy(u, i).wait_recv()
        first = dot(mix_a[u], back[u, :, 0:HALF])
        last = dot(mix_b[u], back[u, :, HALF:])
        for q in range(4):
            h, c = q // 2, (q % 2) * QUART
            mixed = (
                states[u, :, q * QUART : (q + 1) * QUART].astype(F32)
                + first[h * 64 : h * 64 + 32, c : c + QUART]
                + first[h * 64 + 32 : h * 64 + 64, c : c + QUART]
                + last[q * 64 : q * 64 + 32]
                + last[q * 64 + 32 : q * 64 + 64]
            )
            outs[u, :, q * QUART : (q + 1) * QUART] = mixed.astype(BF16)
        out_copy(u).start()

    def out_copy(u):
        return pltpu.make_async_copy(outs.at[u], out_hbm.at[0, u // 2, u % 2], out_sem.at[u])

    def sends(d):
        return sec < sections - 1 if d == 0 else sec > 0

    def takes(d):
        return sec > 0 if d == 0 else sec < sections - 1

    def shift(d):
        @pl.when(sends(d))
        def _():
            h_copy(d).start()

    def arrive(d):
        @pl.when(takes(d))
        def _():
            h_copy(d).wait_recv()

        @pl.when(jnp.logical_not(takes(d)))
        def _():
            (enter_up if d == 0 else enter_down).wait()

    def grad_local():
        turned = dense[...].T
        high, rest = split_two(turned)
        mid, low = split_two(turned - high.astype(F32))
        stacked = jnp.concatenate(
            [high.astype(F32), mid.astype(F32), low.astype(F32), jnp.zeros((8, 4 * TOK), F32)], axis=0
        ).astype(BF16)
        terms = dot(stacked, normed[...])
        gfull[:, 0:D] = terms[0:8] + terms[8:16] + terms[16:24]
        gfull[:, D:] = jnp.zeros((8, 128), F32)
        for p in range(16):
            piece = gfull[:, p * PART : p * PART + 256]
            gsend[p % 2, p // 2] = jnp.concatenate(
                [piece, jnp.zeros((8, 256), F32)], axis=0
            ).astype(BF16)
        g_copy(7).start()

    def grad_share():
        g_copy(7).wait_recv()
        gsum[...] = (gsend[dp].astype(F32) + grecv[...].astype(F32)).astype(BF16)
        for i in range(7):
            g_copy(i).start()
        gall[me] = gsum[me]

    def grad_total():
        for i in range(7):
            g_copy(i).wait_recv()
        grads[0] = jnp.sum(gall[...].astype(F32), axis=0)[0:8, 0:PART]

    turn()
    slots(0)
    loads[0].wait()
    norm(0)
    pack(0)
    pl.semaphore_wait(barrier, 8 + (sec > 0).astype(jnp.int32) + (sec < sections - 1).astype(jnp.int32))
    z_copy(0, 1).start()
    z_copy(0, 0).start()
    y_copy(0, 7).start()
    gath[0, block(me)] = packed[0, block(me)]
    loads[2].wait()
    loads[3].wait()
    z_copy(0, 4).start()
    z_copy(0, 2).start()
    slots(1)
    z_copy(0, 5).start()
    forward(0, 1)
    z_copy(0, 3).start()
    z_copy(0, 6).start()
    loads[1].wait()
    norm(1)
    pack(1)
    z_copy(1, 1).start()
    forward(0, 0)
    y_copy(1, 7).start()
    gath[1, block(me)] = packed[1, block(me)]
    forward(0, 4)
    z_copy(1, 0).start()
    forward(0, 5)
    forward(0, 2)
    z_copy(1, 4).start()
    forward(0, 3)
    z_copy(1, 5).start()
    forward(0, 6)
    forward(1, 1)
    z_copy(1, 6).start()
    z_copy(1, 2).start()
    forward(1, 0)
    compute_own(0)
    compute_other(0)
    s_copy(0, 4).start()
    s_copy(0, 1).start()
    z_copy(1, 3).start()
    s_copy(0, 2).start()
    s_copy(0, 0).start()
    forward(1, 5)
    forward(1, 6)
    give_back(0, 2)
    forward(1, 4)
    forward(1, 3)
    give_back(0, 1)
    forward(1, 2)
    give_back(0, 4)
    give_back(0, 0)
    s_copy(0, 5).start()
    s_copy(0, 6).start()
    compute_own(1)
    s_copy(0, 3).start()
    give_back(0, 5)
    compute_other(1)
    s_copy(1, 0).start()
    give_back(0, 6)
    give_back(0, 3)
    s_copy(0, 7).start()
    s_copy(1, 4).start()
    slots(2)
    s_copy(1, 1).start()
    give_back(1, 0)
    s_copy(1, 2).start()
    gate(0)
    s_copy(1, 3).start()
    s_copy(1, 5).start()
    gate(1)
    give_back(1, 4)
    give_back(0, 7)
    give_back(1, 1)
    s_copy(1, 6).start()
    combine(0)
    shift(0)
    give_back(1, 2)
    give_back(1, 3)
    give_back(1, 5)
    arrive(0)
    norm(2)
    pack(2)
    z_copy(2, 1).start()
    s_copy(1, 7).start()
    z_copy(2, 2).start()
    give_back(1, 6)
    z_copy(2, 3).start()
    give_back(1, 7)
    forward(2, 1)
    z_copy(2, 0).start()
    z_copy(2, 4).start()
    z_copy(2, 5).start()
    y_copy(2, 7).start()
    gath[2, block(me)] = packed[2, block(me)]
    combine(1)
    shift(1)
    forward(2, 2)
    forward(2, 3)
    slots(3)
    z_copy(2, 6).start()
    forward(2, 0)
    arrive(1)
    norm(3)
    pack(3)
    z_copy(3, 0).start()
    z_copy(3, 1).start()
    y_copy(3, 7).start()
    gath[3, block(me)] = packed[3, block(me)]
    z_copy(3, 3).start()
    forward(2, 5)
    forward(2, 4)
    gate(3)
    gate(2)
    z_copy(3, 6).start()
    forward(3, 1)
    forward(2, 6)
    compute_own(2)
    forward(3, 0)
    z_copy(3, 4).start()
    forward(3, 3)
    compute_other(2)
    s_copy(2, 0).start()
    z_copy(3, 5).start()
    z_copy(3, 2).start()
    s_copy(2, 2).start()
    grad_local()
    forward(3, 6)
    s_copy(2, 1).start()
    give_back(2, 0)
    s_copy(2, 4).start()
    grad_share()
    give_back(2, 2)
    forward(3, 4)
    give_back(2, 4)
    forward(3, 5)
    give_back(2, 1)
    forward(3, 2)
    compute_own(3)
    s_copy(2, 3).start()
    s_copy(2, 6).start()
    compute_other(3)
    s_copy(3, 0).start()
    s_copy(3, 1).start()
    s_copy(2, 5).start()
    give_back(2, 3)
    s_copy(3, 4).start()
    s_copy(3, 3).start()
    give_back(3, 0)
    give_back(3, 1)
    s_copy(3, 2).start()
    s_copy(3, 6).start()
    give_back(2, 6)
    s_copy(3, 5).start()
    give_back(3, 4)
    give_back(3, 3)
    give_back(3, 2)
    s_copy(2, 7).start()
    give_back(3, 6)
    give_back(2, 5)
    give_back(3, 5)
    s_copy(3, 7).start()
    grad_total()
    give_back(2, 7)
    combine(2)
    give_back(3, 7)
    combine(3)

    for u in range(UNITS):
        for i in range(7):
            z_copy(u, i).wait_send()
            r_copy(u, i).wait_send()
        for i in range(8):
            y_copy(u, i).wait_send()
            s_copy(u, i).wait_send()
        out_copy(u).wait()
    for i in range(8):
        g_copy(i).wait_send()
    for d in range(2):

        @pl.when(sends(d))
        def _():
            h_copy(d).wait_send()


def per_device(held, entering, gain, router, up, down, routes, cot):
    width = up.shape[-1]
    moved, total = exchange(width, held, entering, gain, router, up, down, routes, cot)
    hbm = pl.BlockSpec(memory_space=pl.ANY)
    return pl.pallas_call(
        settle,
        out_shape=(
            jax.ShapeDtypeStruct(moved.shape, moved.dtype),
            jax.ShapeDtypeStruct(total.shape, total.dtype),
        ),
        in_specs=[hbm, hbm],
        out_specs=(hbm, hbm),
        scratch_shapes=[
            pltpu.VMEM(moved.shape, moved.dtype),
            pltpu.VMEM(total.shape, total.dtype),
            pltpu.SemaphoreType.DMA((UNITS + 1,)),
            pltpu.SemaphoreType.DMA((UNITS + 1,)),
        ],
    )(moved, total)


def settle(moved, total, layer_out, grads, rows, sums, fetch, store):
    pieces = [(moved, rows, layer_out, (0, u // 2, u % 2)) for u in range(UNITS)]
    pieces.append((total, sums, grads, (0,)))
    reads = [
        pltpu.make_async_copy(source.at[at], held.at[at], fetch.at[i])
        for i, (source, held, _, at) in enumerate(pieces)
    ]
    writes = [
        pltpu.make_async_copy(held.at[at], dest.at[at], store.at[i])
        for i, (_, held, dest, at) in enumerate(pieces)
    ]
    for read in reads:
        read.start()
    for read, write in zip(reads, writes):
        read.wait()
        write.start()
    for write in writes:
        write.wait()


def exchange(width, held, entering, gain, router, up, down, routes, cot):
    hbm = pl.BlockSpec(memory_space=pl.ANY)
    vmem = pl.BlockSpec(memory_space=pltpu.VMEM)
    dma = pltpu.SemaphoreType.DMA
    return pl.pallas_call(
        kernel,
        out_shape=(
            jax.ShapeDtypeStruct((1, TICKS, 2, TOK, D), BF16),
            jax.ShapeDtypeStruct((1, NE, PART), F32),
        ),
        in_specs=[hbm, hbm, vmem, vmem, hbm, hbm, vmem, vmem],
        out_specs=(hbm, vmem),
        scratch_shapes=[
            pltpu.VMEM((UNITS, TOK, D), BF16),
            pltpu.VMEM((UNITS * TOK, D), BF16),
            pltpu.VMEM((D, width), BF16),
            pltpu.VMEM((width, D), BF16),
            pltpu.VMEM((UNITS, ROWS, PACK), BF16),
            pltpu.VMEM((UNITS, 2 * ROWS, PACK), BF16),
            pltpu.VMEM((UNITS, 2 * ROWS, PACK), BF16),
            pltpu.VMEM((UNITS, ROWS, PACK), BF16),
            pltpu.VMEM((UNITS, ROWS, PACK), BF16),
            pltpu.VMEM((UNITS, ROWS, PACK), BF16),
            pltpu.VMEM((UNITS, TOK, D), BF16),
            pltpu.VMEM((UNITS, 192, ROWS), F32),
            pltpu.VMEM((UNITS, ROWS, 64), BF16),
            pltpu.VMEM((UNITS, ROWS, ROWS), BF16),
            pltpu.VMEM((UNITS, 128, ROWS), BF16),
            pltpu.VMEM((UNITS, 256, ROWS), BF16),
            pltpu.VMEM((2 * TOK, 2 * UNITS), jnp.int32),
            pltpu.VMEM((TOK, 2 * UNITS), F32),
            pltpu.VMEM((UNITS * TOK, NE), F32),
            pltpu.VMEM((NE, D + 128), F32),
            pltpu.VMEM((2, NE, 16, 256), BF16),
            pltpu.VMEM((NE, 16, 256), BF16),
            pltpu.VMEM((NE, 16, 256), BF16),
            pltpu.VMEM((NE, 16, 256), BF16),
            dma((6,)),
            dma((UNITS,)),
            dma((UNITS, 7)),
            dma((UNITS, 7)),
            dma((UNITS, 8)),
            dma((UNITS, 8)),
            dma((UNITS, 8)),
            dma((UNITS, 8)),
            dma((UNITS, 7)),
            dma((UNITS, 7)),
            dma((2,)),
            dma((2,)),
            dma((8,)),
            dma((8,)),
        ],
        compiler_params=pltpu.CompilerParams(
            collective_id=0, has_side_effects=True, vmem_limit_bytes=56 << 20
        ),
        cost_estimate=pl.CostEstimate(
            flops=12_000_000_000, bytes_accessed=12_000_000, transcendentals=1_000_000
        ),
    )(held, entering, gain, router, up, down, jnp.swapaxes(routes, 3, 4), jnp.swapaxes(cot, 3, 4))


def solution(mesh):
    placed = (
        P("section", None, ("expert", "dp"), None),
        P(None, None, ("expert", "dp"), None),
        P("section", None),
        P("section", None, None),
        P("section", "expert", None, "dp"),
        P("section", "expert", "dp", None),
        P("section", None, None, "expert", None),
        P("section", None, None, ("expert", "dp"), None),
    )
    return jax.shard_map(
        per_device,
        mesh=mesh,
        in_specs=placed,
        out_specs=(
            P("section", None, None, ("expert", "dp"), None),
            P("section", None, ("expert", "dp")),
        ),
        check_vma=False,
    )
```

```python
import functools

import jax
import jax.numpy as jnp
from jax import lax
from jax.experimental import pallas as pl
from jax.experimental.pallas import tpu as pltpu
from jax.sharding import PartitionSpec as P

TICKS = 2
UNITS = 4
D = 3584
TOK = 32
NE = 8
HALF = D // 2
QUART = D // 4
PACK = HALF + QUART
ROWS = NE * 16
PART = D // 16
SCALE = 2.5
MESH = pl.DeviceIdType.MESH
F32 = jnp.float32
BF16 = jnp.bfloat16
RING = (1, 7, 2, 6, 3, 5, 4)
BACK = (4, 3, 5, 2, 6, 1, 7)


def dot(a, b):
    return jnp.dot(a, b, preferred_element_type=F32)


def split_two(value):
    high = value.astype(BF16)
    return high, (value - high.astype(F32)).astype(BF16)


def kernel(
    held,
    entering,
    gain,
    router,
    up_hbm,
    down_hbm,
    routes,
    cot,
    out_hbm,
    grads,
    states,
    normed,
    up,
    down,
    packed,
    gath,
    part,
    yret,
    summed,
    back,
    outs,
    place,
    place_a,
    place_b,
    mix_a,
    mix_b,
    route_rows,
    cot_rows,
    dense,
    gfull,
    gsend,
    grecv,
    gsum,
    gall,
    in_sem,
    out_sem,
    zs,
    zr,
    ys,
    yr,
    ss,
    sr,
    rs,
    rr,
    hs,
    hr,
    gs,
    gr,
):
    sec = lax.axis_index("section")
    me = lax.axis_index("expert")
    dp = lax.axis_index("dp")
    sections = lax.axis_size("section")

    def ring(offset):
        return lax.rem(me + offset + NE, NE)

    def block(index):
        return pl.ds(pl.multiple_of(index * 16, 16), 16)

    def other(index):
        return pl.ds(pl.multiple_of(index * 16 + ROWS, 16), 16)

    barrier = pltpu.get_barrier_semaphore()
    for offset in RING:
        pl.semaphore_signal(barrier, inc=1, device_id={"expert": ring(offset)}, device_id_type=MESH)
    pl.semaphore_signal(barrier, inc=1, device_id={"dp": 1 - dp}, device_id_type=MESH)

    @pl.when(sec > 0)
    def _():
        pl.semaphore_signal(barrier, inc=1, device_id={"section": sec - 1}, device_id_type=MESH)

    @pl.when(sec < sections - 1)
    def _():
        pl.semaphore_signal(barrier, inc=1, device_id={"section": sec + 1}, device_id_type=MESH)

    loads = [
        pltpu.make_async_copy(held.at[0, 0], states.at[0], in_sem.at[0]),
        pltpu.make_async_copy(held.at[0, 1], states.at[1], in_sem.at[1]),
        pltpu.make_async_copy(up_hbm.at[0, 0], up, in_sem.at[2]),
        pltpu.make_async_copy(down_hbm.at[0, 0], down, in_sem.at[3]),
    ]
    loads[0].start()
    loads[1].start()
    enter_up = pltpu.make_async_copy(entering.at[0, 0], states.at[2], in_sem.at[4])
    enter_down = pltpu.make_async_copy(entering.at[0, 1], states.at[3], in_sem.at[5])

    @pl.when(sec == 0)
    def _():
        enter_up.start()

    @pl.when(sec == sections - 1)
    def _():
        enter_down.start()

    def z_copy(u, i):
        to = ring(RING[i])
        return pltpu.make_async_remote_copy(
            src_ref=packed.at[u, block(to)],
            dst_ref=gath.at[u, block(me)],
            send_sem=zs.at[u, i],
            recv_sem=zr.at[u, i],
            device_id={"expert": to},
            device_id_type=MESH,
        )

    def origin(i):
        return me if i == 7 else ring(-RING[i])

    def y_copy(u, i):
        src = packed if i == 7 else gath
        return pltpu.make_async_remote_copy(
            src_ref=src.at[u, block(origin(i))],
            dst_ref=gath.at[u, other(origin(i))],
            send_sem=ys.at[u, i],
            recv_sem=yr.at[u, i],
            device_id={"dp": 1 - dp},
            device_id_type=MESH,
        )

    def target(i):
        return me if i == 7 else ring(BACK[i])

    def s_copy(u, i):
        return pltpu.make_async_remote_copy(
            src_ref=part.at[u, other(target(i))],
            dst_ref=yret.at[u, block(target(i))],
            send_sem=ss.at[u, i],
            recv_sem=sr.at[u, i],
            device_id={"dp": 1 - dp},
            device_id_type=MESH,
        )

    def r_copy(u, i):
        to = ring(BACK[i])
        return pltpu.make_async_remote_copy(
            src_ref=summed.at[u, block(to)],
            dst_ref=back.at[u, block(me)],
            send_sem=rs.at[u, i],
            recv_sem=rr.at[u, i],
            device_id={"expert": to},
            device_id_type=MESH,
        )

    def h_copy(d):
        return pltpu.make_async_remote_copy(
            src_ref=outs.at[d],
            dst_ref=states.at[2 + d],
            send_sem=hs.at[d],
            recv_sem=hr.at[d],
            device_id={"section": sec + 1 if d == 0 else sec - 1},
            device_id_type=MESH,
        )

    def g_copy(i):
        if i == 7:
            return pltpu.make_async_remote_copy(
                src_ref=gsend.at[1 - dp],
                dst_ref=grecv,
                send_sem=gs.at[7],
                recv_sem=gr.at[7],
                device_id={"dp": 1 - dp},
                device_id_type=MESH,
            )
        to = ring(RING[i])
        return pltpu.make_async_remote_copy(
            src_ref=gsum.at[to],
            dst_ref=gall.at[me],
            send_sem=gs.at[i],
            recv_sem=gr.at[i],
            device_id={"expert": to},
            device_id_type=MESH,
        )

    def rows_of(u):
        return slice(u * TOK, (u + 1) * TOK)

    def turn():
        pairs = [(t, d) for t in range(TICKS) for d in range(2)]
        named = jnp.concatenate([routes[0, t, d] for t, d in pairs], axis=0)
        route_rows[...] = named.astype(F32).T.astype(jnp.int32)
        cot_rows[...] = jnp.concatenate([cot[0, t, d] for t, d in pairs], axis=0).T

    def own_routes(u):
        return route_rows[pl.ds(pl.multiple_of(dp * TOK, TOK), TOK), 2 * u : 2 * u + 2]

    def slots(u):
        chosen = own_routes(u)
        lane = lax.broadcasted_iota(jnp.int32, (TOK, ROWS), 1)
        expert, row = lane // 16, lane % 16
        hit = (chosen[:, 0:1] == expert) | (chosen[:, 1:2] == expert)
        earlier = lax.broadcasted_iota(jnp.int32, (TOK, TOK), 0) > lax.broadcasted_iota(
            jnp.int32, (TOK, TOK), 1
        )
        rank = dot(earlier.astype(F32).astype(BF16), hit.astype(F32).astype(BF16)).astype(jnp.int32)
        first = hit & (rank == row % 8)
        last = hit & (rank == 8 + row % 4)
        pa = jnp.concatenate([(first & (row // 8 == h)).astype(F32) for h in range(2)], axis=0)
        pb = jnp.concatenate([(last & (row // 4 == q)).astype(F32) for q in range(4)], axis=0)
        place[u, 0:64] = pa
        place[u, 64:192] = pb
        place_a[u] = pa.T.astype(BF16)
        place_b[u] = pb.T.astype(BF16)

    def norm(u):
        values = states[u].astype(F32)
        meansq = jnp.mean(values * values, axis=-1, keepdims=True)
        normed[rows_of(u)] = (
            values * lax.rsqrt(meansq + 1e-06) * gain[...].astype(F32)
        ).astype(BF16)

    def pack(u):
        own = normed[rows_of(u)]
        halves = jnp.concatenate([own[:, :HALF], own[:, HALF:]], axis=0)
        packed[u, :, 0:HALF] = dot(place_a[u], halves).astype(BF16)
        quarters = jnp.concatenate([own[:, q * QUART : (q + 1) * QUART] for q in range(4)], axis=0)
        packed[u, :, HALF:] = dot(place_b[u], quarters).astype(BF16)

    def dispatch(u):
        for i in range(7):
            z_copy(u, i).start()
        y_copy(u, 7).start()
        gath[u, block(me)] = packed[u, block(me)]

    def forward(u, i):
        z_copy(u, i).wait_recv()
        y_copy(u, i).start()

    def gate(u):
        chosen = own_routes(u)
        cotangent = cot_rows[:, 2 * u : 2 * u + 2]
        logits = lax.dot_general(
            normed[rows_of(u)], router[0], (((1,), (1,)), ((), ())), preferred_element_type=F32
        )
        lane = lax.broadcasted_iota(jnp.int32, (TOK, NE), 1)
        hit0, hit1 = chosen[:, 0:1] == lane, chosen[:, 1:2] == lane
        affinity = jnp.where(hit0 | hit1, jax.nn.sigmoid(logits), 0.0)
        total = jnp.sum(affinity, axis=1, keepdims=True)
        weights = SCALE * affinity / total
        cots = jnp.where(hit0, cotangent[:, 0:1], 0.0) + jnp.where(hit1, cotangent[:, 1:2], 0.0)
        inner = jnp.sum(cots * affinity, axis=1, keepdims=True)
        slope = SCALE * (cots / total - inner / (total * total))
        dense[rows_of(u)] = slope * affinity * (1.0 - affinity)
        expert = lax.broadcasted_iota(jnp.int32, (TOK, ROWS), 1) // 16
        spread = jnp.zeros((TOK, ROWS), F32)
        for e in range(NE):
            spread = jnp.where(expert == e, weights[:, e : e + 1], spread)
        high, low = split_two(spread)
        high, low = high.astype(F32), low.astype(F32)
        for h in range(6):
            hot = place[u, h * TOK : (h + 1) * TOK]
            both = jnp.concatenate([hot * high, hot * low], axis=0).astype(BF16)
            if h < 2:
                mix_a[u, h * 64 : (h + 1) * 64] = both
            else:
                mix_b[u, (h - 2) * 64 : (h - 1) * 64] = both

    def hidden(u, side):
        rows = slice(side * ROWS, side * ROWS + ROWS)
        first = gath[u, rows, 0:HALF]
        left = dot(first, up[0:HALF]).reshape(8, 2, 8, 512)
        right = dot(first, up[HALF:]).reshape(8, 2, 8, 512)
        pre_a = (left[:, 0] + right[:, 1]).reshape(64, 512)
        last = gath[u, rows, HALF:]
        upper = lax.broadcasted_iota(jnp.int32, (8, 8, 512), 1) < 4
        quart = [
            dot(last, up[g * QUART : (g + 1) * QUART]).reshape(8, 2, 8, 512)[:, g // 2]
            for g in range(4)
        ]
        halves = jnp.where(upper, quart[0] + quart[2], quart[1] + quart[3])
        pre_b = (halves + pltpu.roll(halves, 4, 1)).reshape(64, 512)
        pre = jnp.concatenate([pre_a, pre_b], axis=0)
        return (pre * jax.nn.sigmoid(pre)).astype(BF16)

    def project(u, acts, side):
        left = dot(acts, down[:, 0:HALF])
        right = dot(acts, down[:, HALF:])
        rows = slice(side * ROWS, side * ROWS + ROWS)
        first = jnp.concatenate(
            [left[0:64].reshape(8, 8, HALF), right[0:64].reshape(8, 8, HALF)], axis=1
        )
        part[u, rows, 0:HALF] = first.reshape(ROWS, HALF).astype(BF16)
        left_b, right_b = left[64:].reshape(8, 8, HALF), right[64:].reshape(8, 8, HALF)
        upper = lax.broadcasted_iota(jnp.int32, (8, 8, QUART), 1) < 4
        last = jnp.concatenate(
            [
                jnp.where(upper, left_b[:, :, :QUART], left_b[:, :, QUART:]),
                jnp.where(upper, right_b[:, :, :QUART], right_b[:, :, QUART:]),
            ],
            axis=1,
        )
        part[u, rows, HALF:] = last.reshape(ROWS, QUART).astype(BF16)

    def compute_own(u):
        project(u, hidden(u, 0), 0)

    def compute_other(u):
        for i in range(8):
            y_copy(u, i).wait_recv()
        project(u, hidden(u, 1), 1)

    def give_back(u, i):
        s_copy(u, i).wait_recv()
        rows = block(target(i))
        value = (part[u, rows].astype(F32) + yret[u, rows].astype(F32)).astype(BF16)
        if i == 7:
            back[u, rows] = value
        else:
            summed[u, rows] = value
            r_copy(u, i).start()

    def combine(u):
        for i in range(7):
            r_copy(u, i).wait_recv()
        first = dot(mix_a[u], back[u, :, 0:HALF])
        last = dot(mix_b[u], back[u, :, HALF:])
        for q in range(4):
            h, c = q // 2, (q % 2) * QUART
            mixed = (
                states[u, :, q * QUART : (q + 1) * QUART].astype(F32)
                + first[h * 64 : h * 64 + 32, c : c + QUART]
                + first[h * 64 + 32 : h * 64 + 64, c : c + QUART]
                + last[q * 64 : q * 64 + 32]
                + last[q * 64 + 32 : q * 64 + 64]
            )
            outs[u, :, q * QUART : (q + 1) * QUART] = mixed.astype(BF16)
        out_copy(u).start()

    def out_copy(u):
        return pltpu.make_async_copy(outs.at[u], out_hbm.at[0, u // 2, u % 2], out_sem.at[u])

    def sends(d):
        return sec < sections - 1 if d == 0 else sec > 0

    def takes(d):
        return sec > 0 if d == 0 else sec < sections - 1

    def shift(d):
        @pl.when(sends(d))
        def _():
            h_copy(d).start()

    def arrive(d):
        @pl.when(takes(d))
        def _():
            h_copy(d).wait_recv()

        @pl.when(jnp.logical_not(takes(d)))
        def _():
            (enter_up if d == 0 else enter_down).wait()

    def grad_local():
        turned = dense[...].T
        high, rest = split_two(turned)
        mid, low = split_two(turned - high.astype(F32))
        stacked = jnp.concatenate(
            [high.astype(F32), mid.astype(F32), low.astype(F32), jnp.zeros((8, 4 * TOK), F32)], axis=0
        ).astype(BF16)
        terms = dot(stacked, normed[...])
        gfull[:, 0:D] = terms[0:8] + terms[8:16] + terms[16:24]
        gfull[:, D:] = jnp.zeros((8, 128), F32)
        for p in range(16):
            piece = gfull[:, p * PART : p * PART + 256]
            gsend[p % 2, p // 2] = jnp.concatenate(
                [piece, jnp.zeros((8, 256), F32)], axis=0
            ).astype(BF16)
        g_copy(7).start()

    def grad_share():
        g_copy(7).wait_recv()
        gsum[...] = (gsend[dp].astype(F32) + grecv[...].astype(F32)).astype(BF16)
        for i in range(7):
            g_copy(i).start()
        gall[me] = gsum[me]

    def grad_total():
        for i in range(7):
            g_copy(i).wait_recv()
        grads[0] = jnp.sum(gall[...].astype(F32), axis=0)[0:8, 0:PART]

    turn()
    slots(0)
    loads[0].wait()
    loads[2].start()
    loads[3].start()
    norm(0)
    pack(0)
    pl.semaphore_wait(barrier, 8 + (sec > 0).astype(jnp.int32) + (sec < sections - 1).astype(jnp.int32))
    z_copy(0, 1).start()
    z_copy(0, 0).start()
    y_copy(0, 7).start()
    gath[0, block(me)] = packed[0, block(me)]
    loads[2].wait()
    loads[3].wait()
    z_copy(0, 4).start()
    z_copy(0, 2).start()
    slots(1)
    z_copy(0, 5).start()
    forward(0, 1)
    z_copy(0, 3).start()
    z_copy(0, 6).start()
    loads[1].wait()
    norm(1)
    pack(1)
    z_copy(1, 1).start()
    forward(0, 0)
    y_copy(1, 7).start()
    gath[1, block(me)] = packed[1, block(me)]
    forward(0, 4)
    z_copy(1, 0).start()
    forward(0, 5)
    forward(0, 2)
    z_copy(1, 4).start()
    forward(0, 3)
    z_copy(1, 5).start()
    forward(0, 6)
    forward(1, 1)
    z_copy(1, 6).start()
    z_copy(1, 2).start()
    forward(1, 0)
    compute_own(0)
    compute_other(0)
    s_copy(0, 4).start()
    s_copy(0, 1).start()
    z_copy(1, 3).start()
    s_copy(0, 2).start()
    s_copy(0, 0).start()
    forward(1, 5)
    forward(1, 6)
    give_back(0, 2)
    forward(1, 4)
    forward(1, 3)
    give_back(0, 1)
    forward(1, 2)
    give_back(0, 4)
    give_back(0, 0)
    s_copy(0, 5).start()
    s_copy(0, 6).start()
    compute_own(1)
    s_copy(0, 3).start()
    give_back(0, 5)
    compute_other(1)
    s_copy(1, 0).start()
    give_back(0, 6)
    give_back(0, 3)
    s_copy(0, 7).start()
    s_copy(1, 4).start()
    slots(2)
    s_copy(1, 1).start()
    give_back(1, 0)
    s_copy(1, 2).start()
    gate(0)
    s_copy(1, 3).start()
    s_copy(1, 5).start()
    gate(1)
    give_back(1, 4)
    give_back(0, 7)
    give_back(1, 1)
    s_copy(1, 6).start()
    combine(0)
    shift(0)
    give_back(1, 2)
    give_back(1, 3)
    give_back(1, 5)
    arrive(0)
    norm(2)
    pack(2)
    z_copy(2, 1).start()
    s_copy(1, 7).start()
    z_copy(2, 2).start()
    give_back(1, 6)
    z_copy(2, 3).start()
    give_back(1, 7)
    forward(2, 1)
    z_copy(2, 0).start()
    z_copy(2, 4).start()
    z_copy(2, 5).start()
    y_copy(2, 7).start()
    gath[2, block(me)] = packed[2, block(me)]
    combine(1)
    shift(1)
    forward(2, 2)
    forward(2, 3)
    slots(3)
    z_copy(2, 6).start()
    forward(2, 0)
    arrive(1)
    norm(3)
    pack(3)
    z_copy(3, 0).start()
    z_copy(3, 1).start()
    y_copy(3, 7).start()
    gath[3, block(me)] = packed[3, block(me)]
    z_copy(3, 3).start()
    forward(2, 5)
    forward(2, 4)
    gate(3)
    gate(2)
    z_copy(3, 6).start()
    forward(3, 1)
    forward(2, 6)
    compute_own(2)
    forward(3, 0)
    z_copy(3, 4).start()
    forward(3, 3)
    compute_other(2)
    s_copy(2, 0).start()
    z_copy(3, 5).start()
    z_copy(3, 2).start()
    s_copy(2, 2).start()
    grad_local()
    forward(3, 6)
    s_copy(2, 1).start()
    give_back(2, 0)
    s_copy(2, 4).start()
    grad_share()
    give_back(2, 2)
    forward(3, 4)
    give_back(2, 4)
    forward(3, 5)
    give_back(2, 1)
    forward(3, 2)
    compute_own(3)
    s_copy(2, 3).start()
    s_copy(2, 6).start()
    compute_other(3)
    s_copy(3, 0).start()
    s_copy(3, 1).start()
    s_copy(2, 5).start()
    give_back(2, 3)
    s_copy(3, 4).start()
    s_copy(3, 3).start()
    give_back(3, 0)
    give_back(3, 1)
    s_copy(3, 2).start()
    s_copy(3, 6).start()
    give_back(2, 6)
    s_copy(3, 5).start()
    give_back(3, 4)
    give_back(3, 3)
    give_back(3, 2)
    s_copy(2, 7).start()
    give_back(3, 6)
    give_back(2, 5)
    give_back(3, 5)
    s_copy(3, 7).start()
    grad_total()
    give_back(2, 7)
    combine(2)
    give_back(3, 7)
    combine(3)

    for u in range(UNITS):
        for i in range(7):
            z_copy(u, i).wait_send()
            r_copy(u, i).wait_send()
        for i in range(8):
            y_copy(u, i).wait_send()
            s_copy(u, i).wait_send()
        out_copy(u).wait()
    for i in range(8):
        g_copy(i).wait_send()
    for d in range(2):

        @pl.when(sends(d))
        def _():
            h_copy(d).wait_send()


def per_device(held, entering, gain, router, up, down, routes, cot):
    width = up.shape[-1]
    moved, total = exchange(width, held, entering, gain, router, up, down, routes, cot)
    hbm = pl.BlockSpec(memory_space=pl.ANY)
    return pl.pallas_call(
        settle,
        out_shape=(
            jax.ShapeDtypeStruct(moved.shape, moved.dtype),
            jax.ShapeDtypeStruct(total.shape, total.dtype),
        ),
        in_specs=[hbm, hbm],
        out_specs=(hbm, hbm),
        scratch_shapes=[
            pltpu.VMEM(moved.shape, moved.dtype),
            pltpu.VMEM(total.shape, total.dtype),
            pltpu.SemaphoreType.DMA((UNITS + 1,)),
            pltpu.SemaphoreType.DMA((UNITS + 1,)),
        ],
    )(moved, total)


def settle(moved, total, layer_out, grads, rows, sums, fetch, store):
    pieces = [(moved, rows, layer_out, (0, u // 2, u % 2)) for u in range(UNITS)]
    pieces.append((total, sums, grads, (0,)))
    reads = [
        pltpu.make_async_copy(source.at[at], held.at[at], fetch.at[i])
        for i, (source, held, _, at) in enumerate(pieces)
    ]
    writes = [
        pltpu.make_async_copy(held.at[at], dest.at[at], store.at[i])
        for i, (_, held, dest, at) in enumerate(pieces)
    ]
    for read in reads:
        read.start()
    for read, write in zip(reads, writes):
        read.wait()
        write.start()
    for write in writes:
        write.wait()


def exchange(width, held, entering, gain, router, up, down, routes, cot):
    hbm = pl.BlockSpec(memory_space=pl.ANY)
    vmem = pl.BlockSpec(memory_space=pltpu.VMEM)
    dma = pltpu.SemaphoreType.DMA
    return pl.pallas_call(
        kernel,
        out_shape=(
            jax.ShapeDtypeStruct((1, TICKS, 2, TOK, D), BF16),
            jax.ShapeDtypeStruct((1, NE, PART), F32),
        ),
        in_specs=[hbm, hbm, vmem, vmem, hbm, hbm, vmem, vmem],
        out_specs=(hbm, vmem),
        scratch_shapes=[
            pltpu.VMEM((UNITS, TOK, D), BF16),
            pltpu.VMEM((UNITS * TOK, D), BF16),
            pltpu.VMEM((D, width), BF16),
            pltpu.VMEM((width, D), BF16),
            pltpu.VMEM((UNITS, ROWS, PACK), BF16),
            pltpu.VMEM((UNITS, 2 * ROWS, PACK), BF16),
            pltpu.VMEM((UNITS, 2 * ROWS, PACK), BF16),
            pltpu.VMEM((UNITS, ROWS, PACK), BF16),
            pltpu.VMEM((UNITS, ROWS, PACK), BF16),
            pltpu.VMEM((UNITS, ROWS, PACK), BF16),
            pltpu.VMEM((UNITS, TOK, D), BF16),
            pltpu.VMEM((UNITS, 192, ROWS), F32),
            pltpu.VMEM((UNITS, ROWS, 64), BF16),
            pltpu.VMEM((UNITS, ROWS, ROWS), BF16),
            pltpu.VMEM((UNITS, 128, ROWS), BF16),
            pltpu.VMEM((UNITS, 256, ROWS), BF16),
            pltpu.VMEM((2 * TOK, 2 * UNITS), jnp.int32),
            pltpu.VMEM((TOK, 2 * UNITS), F32),
            pltpu.VMEM((UNITS * TOK, NE), F32),
            pltpu.VMEM((NE, D + 128), F32),
            pltpu.VMEM((2, NE, 16, 256), BF16),
            pltpu.VMEM((NE, 16, 256), BF16),
            pltpu.VMEM((NE, 16, 256), BF16),
            pltpu.VMEM((NE, 16, 256), BF16),
            dma((6,)),
            dma((UNITS,)),
            dma((UNITS, 7)),
            dma((UNITS, 7)),
            dma((UNITS, 8)),
            dma((UNITS, 8)),
            dma((UNITS, 8)),
            dma((UNITS, 8)),
            dma((UNITS, 7)),
            dma((UNITS, 7)),
            dma((2,)),
            dma((2,)),
            dma((8,)),
            dma((8,)),
        ],
        compiler_params=pltpu.CompilerParams(
            collective_id=0, has_side_effects=True, vmem_limit_bytes=56 << 20
        ),
        cost_estimate=pl.CostEstimate(
            flops=12_000_000_000, bytes_accessed=12_000_000, transcendentals=1_000_000
        ),
    )(held, entering, gain, router, up, down, jnp.swapaxes(routes, 3, 4), jnp.swapaxes(cot, 3, 4))


def solution(mesh):
    placed = (
        P("section", None, ("expert", "dp"), None),
        P(None, None, ("expert", "dp"), None),
        P("section", None),
        P("section", None, None),
        P("section", "expert", None, "dp"),
        P("section", "expert", "dp", None),
        P("section", None, None, "expert", None),
        P("section", None, None, ("expert", "dp"), None),
    )
    return jax.shard_map(
        per_device,
        mesh=mesh,
        in_specs=placed,
        out_specs=(
            P("section", None, None, ("expert", "dp"), None),
            P("section", None, ("expert", "dp")),
        ),
        check_vma=False,
    )
```
